32 devices in a mesh: dp: 8 (over z, x), seq: 4 (over y, core).
Axes of the slice: x: 2, y: 2, z: 4, core: 2. Of those that a mesh axis runs over, the one named last changes fastest.
Arguments:
- queries: bfloat16 [8192, 2560], P(('dp', 'seq')), may hold values from -200 to 200
- keys: bfloat16 [8192, 2560], P(('dp', 'seq')), may hold values from -200 to 200
- values: bfloat16 [8192, 2560], P(('dp', 'seq')), may hold values from -6 to 6
- gain_q: float32 [2560], replicated, may hold values from 0.5 to 1.5
- gain_k: float32 [2560], replicated, may hold values from 0.5 to 1.5
- tile_pairs: int32 [16, 8], replicated, may hold values from 0 to 15, as said below
- tile_lens: int32 [8, 16], P('dp'), may hold values from 40 to 64
- out_grad: bfloat16 [8192, 5120], P(('dp', 'seq')), may hold values from -6 to 6
- w_out: bfloat16 [5120, 2560], P('dp', 'seq'), may hold values from -0.125 to 0.125
Outputs:
- grad_q: bfloat16 [8192, 2560], P(('dp', 'seq'))
- grad_k: bfloat16 [8192, 2560], P(('dp', 'seq'))
- grad_v: bfloat16 [8192, 2560], P(('dp', 'seq'))
- grad_w: float32 [5120, 2560], P('dp', 'seq')
The draws below stay inside these ranges and needn't reach their ends.
Inputs may be any that keep to these rules, and one draw needn't show every extreme that they name: `tile_pairs`: row a lists 8 different tiles of the window, with tile a first.
All inputs are finite; a program needn't handle non-finite values.
Results may differ from the reference program's by a relative error of at most 0.02.
Values may be sent and summed in bfloat16 or wider, within the bound.
A program may use at most 128 MiB of HBM per device.

```python
import math
import jax
import jax.numpy as jnp
from jax import lax

D = 5120
HEAD_DIM = 128
HEADS = 20
TILE = 64
TILES = 16
NEIGH = 8
CLIP_TOK = 1024
HD = 2560
TOKENS = 8192
N_DP = 8


def field_pair(key):
    queries = jnp.clip(jax.random.normal(jax.random.fold_in(key, 101), (TOKENS, HD), jnp.float32), -6.0, 6.0)
    keys = jnp.clip(jax.random.normal(jax.random.fold_in(key, 202), (TOKENS, HD), jnp.float32), -6.0, 6.0)
    return (queries, keys)


def draw_queries(key, part):
    return field_pair(key)[0].astype(jnp.bfloat16)


def draw_keys(key, part):
    return field_pair(key)[1].astype(jnp.bfloat16)


def draw_tile_pairs(key, part):
    row_keys = jax.random.split(jax.random.fold_in(key, 909), TILES)

    def one_row(row_key, index):
        others = jax.random.permutation(row_key, TILES - 1)[:NEIGH - 1].astype(jnp.int32)
        others = jnp.where(others >= index, others + 1, others)
        return jnp.concatenate([index[None], others]).astype(jnp.int32)
    return jax.vmap(one_row)(row_keys, jnp.arange(TILES, dtype=jnp.int32))


def touch_ends(drawn, stream_key, smallest, largest):
    shape = drawn.shape
    place = [jax.random.randint(jax.random.fold_in(stream_key, axis), (), 0, shape[axis]) for axis in range(len(shape))]
    drawn = drawn.at[tuple(place)].set(smallest)
    longest = shape.index(max(shape))
    place[longest] = (place[longest] + 1) % shape[longest]
    return drawn.at[tuple(place)].set(largest)


def strengthened(entries, key, source, target, shards_of, factor):
    def block_of(dim):
        return (jnp.arange(entries.shape[dim]) // (entries.shape[dim] // shards_of)).reshape((-1,) + (1,) * (entries.ndim - 1 - dim))

    first = jax.random.permutation(key, shards_of)[block_of(target)]
    other_side = (block_of(target) + shards_of // 2) % shards_of
    return jnp.where((block_of(source) == first) | (block_of(source) == other_side), factor * entries, entries)


def block_scale(stream_key, shape, shards, least, high):
    def one(position, shards_of):
        steps = jax.random.uniform(jax.random.fold_in(jax.random.fold_in(stream_key, 6), position), (shards_of,), jnp.float32, least / len(shards), high / len(shards))
        return jnp.repeat(jnp.exp(steps), shape[position] // shards_of).reshape((-1,) + (1,) * (len(shape) - position - 1))

    level = one(*shards[0])
    for cut in shards[1:]:
        level = level * one(*cut)
    return level


def gaussian(key, extent, scale, most, cuts=(), held_as=jnp.bfloat16):
    factor_of = block_scale(key, extent, cuts, -0.22, 0.18) if cuts else 1.0
    result = jax.random.normal(key, extent, jnp.float32) * scale * factor_of
    return jnp.minimum(jnp.maximum(result, -most), most).astype(held_as)


def gaussian_with(rng, shape, deviation, most, shards, heavy, kind=jnp.bfloat16):
    entries = deviation * jax.random.normal(rng, shape, jnp.float32)
    if shards:
        entries = entries * block_scale(rng, shape, shards, -0.22, 0.18)
    return jnp.clip(strengthened(entries, jax.random.fold_in(rng, 3), *heavy), -most, most).astype(kind)


def setup_inputs(seed: int = 0) -> dict:
    streams_of = jax.random.split(jax.random.key(seed), 10)
    queries = draw_queries(jax.random.fold_in(streams_of[9], 71), 0)
    keys = draw_keys(jax.random.fold_in(streams_of[9], 71), 0)
    values = gaussian(streams_of[2], (TOKENS, HD), 1.0, 6.0, ((0, 32),))
    gain_q = jnp.clip(1.0 + 0.1 * jax.random.normal(streams_of[3], (HD,), jnp.float32), 0.5, 1.5)
    gain_k = jnp.clip(1.0 + 0.1 * jax.random.normal(streams_of[4], (HD,), jnp.float32), 0.5, 1.5)
    tile_pairs = draw_tile_pairs(jax.random.fold_in(streams_of[9], 71), 0)
    tile_lens = touch_ends(jax.random.randint(streams_of[6], (N_DP, TILES), TILE * 5 // 8, TILE + 1), jax.random.fold_in(streams_of[6], 1), TILE * 5 // 8, TILE).astype(jnp.int32)
    out_grad = gaussian_with(streams_of[7], (TOKENS, D), 1.0, 6.0, ((0, 32),), (0, 1, 32, 2.75))
    w_out = gaussian(streams_of[8], (D, HD), HD ** -0.5, 0.125, ((0, 8), (1, 4)))
    return dict(queries=queries, keys=keys, values=values, gain_q=gain_q, gain_k=gain_k, tile_pairs=tile_pairs, tile_lens=tile_lens, out_grad=out_grad, w_out=w_out)


EPS = 1e-06

def multiply(pattern, left, right):
    return jnp.einsum(pattern, left.astype(jnp.float32), right.astype(jnp.float32), precision=lax.Precision.HIGHEST)

def normalize(field, gain):
    values_f = field.astype(jnp.float32)
    row_scale = lax.rsqrt(lax.optimization_barrier(jnp.mean(values_f * values_f, axis=-1, keepdims=True)) + EPS)
    return ((values_f * row_scale * gain.astype(jnp.float32)).astype(jnp.bfloat16), row_scale)

def norm_back(field, row_scale, gain, grad_normed):
    values_f = field.astype(jnp.float32)
    gated = gain.astype(jnp.float32) * grad_normed.astype(jnp.float32)
    inner = lax.optimization_barrier(jnp.sum(gated * values_f, axis=-1, keepdims=True))
    return (row_scale * gated - values_f * row_scale ** 3 * inner / field.shape[-1]).astype(jnp.bfloat16)

def tile_attention(query_tiles, key_tiles, value_tiles, grad_tiles, tile_pairs, live_lengths):
    tile_count, tile_rows, head_width = query_tiles.shape
    neighbours = tile_pairs.shape[1]
    factor = 1.0 / math.sqrt(head_width)
    key_near = jnp.take(key_tiles, tile_pairs, axis=0).reshape(tile_count, neighbours * tile_rows, head_width)
    value_near = jnp.take(value_tiles, tile_pairs, axis=0).reshape(tile_count, neighbours * tile_rows, head_width)
    near_lengths = jnp.take(live_lengths, tile_pairs, axis=0)
    live = (jnp.arange(tile_rows, dtype=jnp.int32)[None, None, :] < near_lengths[:, :, None]).reshape(tile_count, neighbours * tile_rows)
    scores = multiply('aqd,akd->aqk', query_tiles, key_near) * factor
    scores = jnp.where(live[:, None, :], scores, -jnp.inf)
    row_max = lax.optimization_barrier(jnp.max(scores, axis=-1, keepdims=True))
    weights = jnp.exp(scores - row_max)
    probs = weights / lax.optimization_barrier(jnp.sum(weights, axis=-1, keepdims=True))
    probs_low = probs.astype(jnp.bfloat16)
    attended = multiply('aqk,akd->aqd', probs_low, value_near).astype(jnp.bfloat16)
    grad_probs = multiply('aqd,akd->aqk', grad_tiles, value_near)
    delta = lax.optimization_barrier(jnp.sum(probs * grad_probs, axis=-1, keepdims=True))
    grad_scores = (probs * (grad_probs - delta)).astype(jnp.bfloat16)
    grad_query = (multiply('aqk,akd->aqd', grad_scores, key_near) * factor).astype(jnp.bfloat16)
    grad_key_near = multiply('aqk,aqd->akd', grad_scores, query_tiles) * factor
    grad_value_near = multiply('aqk,aqd->akd', probs_low, grad_tiles)
    owners = (tile_pairs[:, :, None] == jnp.arange(tile_count, dtype=jnp.int32)[None, None, :]).astype(jnp.float32)
    grad_key = jnp.einsum('anb,antd->btd', owners, grad_key_near.reshape(tile_count, neighbours, tile_rows, head_width), precision=lax.Precision.HIGHEST).astype(jnp.bfloat16)
    grad_value = jnp.einsum('anb,antd->btd', owners, grad_value_near.reshape(tile_count, neighbours, tile_rows, head_width), precision=lax.Precision.HIGHEST).astype(jnp.bfloat16)
    return (attended, grad_query, grad_key, grad_value)

def reference(queries, keys, values, gain_q, gain_k, tile_pairs, tile_lens, out_grad, w_out):

    def split(field):
        return field.reshape(TILES, TILE, HEADS, HEAD_DIM).transpose(2, 0, 1, 3)

    def merge(field):
        return field.transpose(1, 2, 0, 3).reshape(CLIP_TOK, HD)

    def one_clip(running, inputs):
        clip_query, clip_key, clip_value, clip_grad, clip_lengths = inputs
        query_normed, query_scale = normalize(clip_query, gain_q)
        key_normed, key_scale = normalize(clip_key, gain_k)
        grad_attended = jnp.dot(clip_grad, w_out, preferred_element_type=jnp.float32).astype(jnp.bfloat16)

        def one_head(group):
            return tile_attention(group[0], group[1], group[2], group[3], tile_pairs, clip_lengths)
        attended, grad_qn, grad_kn, grad_vh = lax.map(one_head, (split(query_normed), split(key_normed), split(clip_value), split(grad_attended)))
        attended = merge(attended)
        running = running + jnp.dot(clip_grad.T, attended, preferred_element_type=jnp.float32) / N_DP
        grad_query = norm_back(clip_query, query_scale, gain_q, merge(grad_qn))
        grad_key = norm_back(clip_key, key_scale, gain_k, merge(grad_kn))
        return (running, (grad_query, grad_key, merge(grad_vh)))
    clips = (queries.reshape(N_DP, CLIP_TOK, HD), keys.reshape(N_DP, CLIP_TOK, HD), values.reshape(N_DP, CLIP_TOK, HD), out_grad.reshape(N_DP, CLIP_TOK, D), tile_lens)
    grad_w, stacked = lax.scan(one_clip, jnp.zeros((D, HD), jnp.float32), clips)
    grad_q = stacked[0].reshape(TOKENS, HD)
    grad_k = stacked[1].reshape(TOKENS, HD)
    grad_v = stacked[2].reshape(TOKENS, HD)
    return (grad_q, grad_k, grad_v, grad_w)
```

```python
import functools
import math

import jax
import jax.numpy as jnp
from jax import lax
from jax.experimental import pallas as pl
from jax.experimental.pallas import tpu as pltpu
from jax.sharding import PartitionSpec as P

HEAD_DIM = 128
BLOCK_Q = 256
EPS = 1e-06
DEAD = -1e30
VMEM_LIMIT = 48 * 1024 * 1024


def normalize(field, gain):
    values_f = field.astype(jnp.float32)
    row_scale = lax.rsqrt(jnp.mean(values_f * values_f, axis=-1, keepdims=True) + EPS)
    return ((values_f * row_scale * gain).astype(jnp.bfloat16), row_scale)


def norm_finish(values_f, row_scale, gated, inner, width):
    return (row_scale * gated - values_f * row_scale**3 * inner / width).astype(jnp.bfloat16)


def dot_nt(left, right):
    return lax.dot_general(
        left, right, (((1,), (1,)), ((), ())), preferred_element_type=jnp.float32
    )


def dot_nn(left, right):
    return jnp.dot(left, right, preferred_element_type=jnp.float32)


def forward_kernel(factor, q_ref, k_ref, v_ref, bias_ref, probs_ref, out_ref):
    scores = dot_nt(k_ref[...], q_ref[...]) * factor + bias_ref[...].astype(jnp.float32)
    weights = jnp.exp(scores - jnp.max(scores, axis=0, keepdims=True))
    probs = weights * (1.0 / jnp.sum(weights, axis=0, keepdims=True))
    probs_low = probs.astype(jnp.bfloat16)
    probs_ref[0] = probs_low
    attended = dot_nn(v_ref[...].T, probs_low)
    out_ref[...] = attended.T.astype(jnp.bfloat16)


def backward_kernel(
    factor, q_ref, k_ref, v_ref, g_ref, probs_ref, dq_ref, dk_ref, dv_ref, dk_sum, dv_sum
):
    block = pl.program_id(1)

    @pl.when(block == 0)
    def _():
        dk_sum[...] = jnp.zeros_like(dk_sum)
        dv_sum[...] = jnp.zeros_like(dv_sum)

    grad = g_ref[...]
    probs_low = probs_ref[0]
    dv_sum[...] += dot_nn(probs_low, grad)
    grad_probs = dot_nt(v_ref[...], grad)
    probs = probs_low.astype(jnp.float32)
    delta = jnp.sum(probs * grad_probs, axis=0, keepdims=True)
    grad_scores = (probs * (grad_probs - delta)).astype(jnp.bfloat16)
    dk_sum[...] += dot_nn(grad_scores, q_ref[...])
    dq_ref[...] = (dot_nn(k_ref[...].T, grad_scores) * factor).T.astype(jnp.bfloat16)

    @pl.when(block == pl.num_programs(1) - 1)
    def _():
        dk_ref[...] = (dk_sum[...] * factor).astype(jnp.bfloat16)
        dv_ref[...] = dv_sum[...].astype(jnp.bfloat16)


def attention_forward(query, key, value, bias):
    rows, width = query.shape
    heads = width // HEAD_DIM
    blocks = rows // BLOCK_Q
    by_query = pl.BlockSpec((BLOCK_Q, HEAD_DIM), lambda h, b: (b, h))
    by_key = pl.BlockSpec((rows, HEAD_DIM), lambda h, b: (0, h))
    pairs = heads * rows * rows
    return pl.pallas_call(
        functools.partial(forward_kernel, 1.0 / math.sqrt(HEAD_DIM)),
        grid=(heads, blocks),
        in_specs=[by_query, by_key, by_key, pl.BlockSpec((rows, BLOCK_Q), lambda h, b: (0, b))],
        out_specs=[pl.BlockSpec((1, rows, BLOCK_Q), lambda h, b: (h, 0, b)), by_query],
        out_shape=[
            jax.ShapeDtypeStruct((heads, rows, rows), jnp.bfloat16),
            jax.ShapeDtypeStruct((rows, width), jnp.bfloat16),
        ],
        compiler_params=pltpu.CompilerParams(vmem_limit_bytes=VMEM_LIMIT),
        cost_estimate=pl.CostEstimate(
            flops=4 * pairs * HEAD_DIM, bytes_accessed=4 * pairs, transcendentals=pairs
        ),
        name="attention_forward",
    )(query, key, value, bias)


def attention_backward(query, key, value, grad, probs):
    rows, width = query.shape
    heads = width // HEAD_DIM
    blocks = rows // BLOCK_Q
    by_query = pl.BlockSpec((BLOCK_Q, HEAD_DIM), lambda h, b: (b, h))
    by_key = pl.BlockSpec((rows, HEAD_DIM), lambda h, b: (0, h))
    pairs = heads * rows * rows
    shape = jax.ShapeDtypeStruct((rows, width), jnp.bfloat16)
    return pl.pallas_call(
        functools.partial(backward_kernel, 1.0 / math.sqrt(HEAD_DIM)),
        grid=(heads, blocks),
        in_specs=[
            by_query,
            by_key,
            by_key,
            by_query,
            pl.BlockSpec((1, rows, BLOCK_Q), lambda h, b: (h, 0, b)),
        ],
        out_specs=[by_query, by_key, by_key],
        out_shape=[shape, shape, shape],
        scratch_shapes=[
            pltpu.VMEM((rows, HEAD_DIM), jnp.float32),
            pltpu.VMEM((rows, HEAD_DIM), jnp.float32),
        ],
        compiler_params=pltpu.CompilerParams(vmem_limit_bytes=VMEM_LIMIT),
        cost_estimate=pl.CostEstimate(
            flops=8 * pairs * HEAD_DIM, bytes_accessed=4 * pairs, transcendentals=0
        ),
        name="attention_backward",
    )(query, key, value, grad, probs)


def score_bias(tile_pairs, clip_lengths, clip_rows):
    tile_count = tile_pairs.shape[0]
    tile_rows = clip_rows // tile_count
    tiles = jnp.arange(tile_count, dtype=jnp.int32)
    listed = jnp.any(tile_pairs[:, :, None] == tiles[None, None, :], axis=1)
    lengths = jnp.where(listed, clip_lengths[None, :], 0)
    live = jnp.arange(tile_rows, dtype=jnp.int32)[None, :, None] < lengths.T[:, None, :]
    bias = jnp.where(live, 0.0, DEAD).astype(jnp.bfloat16).reshape(clip_rows, tile_count)
    return jnp.repeat(bias, tile_rows, axis=1)


def per_device(queries, keys, values, gain_q, gain_k, tile_pairs, tile_lens, out_grad, w_out):
    dp_count = lax.axis_size("dp")
    width = queries.shape[1]
    clip_rows = queries.shape[0] * lax.axis_size("seq")
    w_all = lax.all_gather(w_out, "dp", axis=0, tiled=True)
    cot_all = lax.all_gather(out_grad, "seq", axis=0, tiled=True)
    query_normed, query_scale = normalize(queries, gain_q)
    key_normed, key_scale = normalize(keys, gain_k)
    query_heads, key_heads, value_heads = (
        lax.all_to_all(query_normed, "seq", split_axis=1, concat_axis=0, tiled=True),
        lax.all_to_all(key_normed, "seq", split_axis=1, concat_axis=0, tiled=True),
        lax.all_to_all(values, "seq", split_axis=1, concat_axis=0, tiled=True),
    )
    bias = score_bias(tile_pairs, tile_lens[0], clip_rows)
    probs, attended = attention_forward(query_heads, key_heads, value_heads, bias)
    partial_w = (
        lax.dot_general(
            cot_all, attended, (((0,), (0,)), ((), ())), preferred_element_type=jnp.float32
        )
        / dp_count
    ).astype(jnp.bfloat16)
    grad_w = lax.psum_scatter(partial_w, "dp", scatter_dimension=0, tiled=True)
    grad_attended = dot_nn(cot_all, w_all).astype(jnp.bfloat16)
    grad_qn, grad_kn, grad_vh = attention_backward(
        query_heads, key_heads, value_heads, grad_attended, probs
    )
    grad_qt, grad_kt, grad_v = (
        lax.all_to_all(grad_qn, "seq", split_axis=0, concat_axis=1, tiled=True),
        lax.all_to_all(grad_kn, "seq", split_axis=0, concat_axis=1, tiled=True),
        lax.all_to_all(grad_vh, "seq", split_axis=0, concat_axis=1, tiled=True),
    )
    query_full = queries.astype(jnp.float32)
    key_full = keys.astype(jnp.float32)
    gated_q = gain_q * grad_qt.astype(jnp.float32)
    gated_k = gain_k * grad_kt.astype(jnp.float32)
    inner_q = jnp.sum(gated_q * query_full, axis=-1, keepdims=True)
    inner_k = jnp.sum(gated_k * key_full, axis=-1, keepdims=True)
    grad_q = norm_finish(query_full, query_scale, gated_q, inner_q, width)
    grad_k = norm_finish(key_full, key_scale, gated_k, inner_k, width)
    return (grad_q, grad_k, grad_v, grad_w.astype(jnp.float32))


def solution(mesh):
    return jax.shard_map(
        per_device,
        mesh=mesh,
        in_specs=(
            P(("dp", "seq"), None),
            P(("dp", "seq"), None),
            P(("dp", "seq"), None),
            P(),
            P(),
            P(),
            P("dp", None),
            P(("dp", "seq"), None),
            P("dp", "seq"),
        ),
        out_specs=(
            P(("dp", "seq"), None),
            P(("dp", "seq"), None),
            P(("dp", "seq"), None),
            P("dp", "seq"),
        ),
        check_vma=False,
    )
```

```python
import functools
import math

import jax
import jax.numpy as jnp
from jax import lax
from jax.experimental import pallas as pl
from jax.experimental.pallas import tpu as pltpu
from jax.sharding import PartitionSpec as P

HEAD_DIM = 128
ROW_BLOCK = 64
EPS = 1e-06
DEAD = -1e30
VMEM_LIMIT = 48 * 1024 * 1024


def dot_nt(left, right):
    return lax.dot_general(
        left, right, (((1,), (1,)), ((), ())), preferred_element_type=jnp.float32
    )


def dot_tn(left, right):
    return lax.dot_general(
        left, right, (((0,), (0,)), ((), ())), preferred_element_type=jnp.float32
    )


def dot_nn(left, right):
    return jnp.dot(left, right, preferred_element_type=jnp.float32)


def columns_of(owner, width):
    return pl.ds(pl.multiple_of(owner * width, HEAD_DIM), width)


def prepare_kernel(me_ref, q_ref, k_ref, v_ref, gain_q_ref, gain_k_ref, *rest):
    sends, held = rest[:-1], rest[-1]
    for which, (field_ref, gain_ref) in enumerate(((q_ref, gain_q_ref), (k_ref, gain_k_ref))):
        values_f = field_ref[...].astype(jnp.float32)
        row_scale = lax.rsqrt(jnp.mean(values_f * values_f, axis=-1, keepdims=True) + EPS)
        held[which] = (values_f * row_scale * gain_ref[...]).astype(jnp.bfloat16)
    held[2] = v_ref[...]
    for step, send_ref in enumerate(sends):
        part = columns_of(me_ref[0] ^ step, send_ref.shape[2])
        for which in range(3):
            send_ref[which] = held[which, :, part]


def prepare(me, queries, keys, values, gain_q, gain_k, peers):
    rows, width = queries.shape
    part = width // peers
    by_row = pl.BlockSpec((ROW_BLOCK, width), lambda i, me: (i, 0))
    gain = pl.BlockSpec((1, width), lambda i, me: (0, 0))
    return pl.pallas_call(
        prepare_kernel,
        grid_spec=pltpu.PrefetchScalarGridSpec(
            num_scalar_prefetch=1,
            grid=(rows // ROW_BLOCK,),
            in_specs=[by_row, by_row, by_row, gain, gain],
            out_specs=[pl.BlockSpec((3, ROW_BLOCK, part), lambda i, me: (0, i, 0))] * peers,
            scratch_shapes=[pltpu.VMEM((3, ROW_BLOCK, width), jnp.bfloat16)],
        ),
        out_shape=[jax.ShapeDtypeStruct((3, rows, part), jnp.bfloat16)] * peers,
        compiler_params=pltpu.CompilerParams(vmem_limit_bytes=VMEM_LIMIT),
        name="prepare",
    )(me, queries, keys, values, gain_q[None], gain_k[None])


def finish_kernel(me_ref, q_ref, k_ref, gain_q_ref, gain_k_ref, *rest):
    parts, (dq_ref, dk_ref, dv_ref, held) = rest[:-4], rest[-4:]
    for step, part_ref in enumerate(parts):
        part = columns_of(me_ref[0] ^ step, part_ref.shape[2])
        held[0, :, part] = part_ref[0]
        held[1, :, part] = part_ref[1]
        dv_ref[:, part] = part_ref[2]
    for which, (field_ref, gain_ref, out_ref) in enumerate(
        ((q_ref, gain_q_ref, dq_ref), (k_ref, gain_k_ref, dk_ref))
    ):
        values_f = field_ref[...].astype(jnp.float32)
        width = values_f.shape[1]
        row_scale = lax.rsqrt(jnp.mean(values_f * values_f, axis=-1, keepdims=True) + EPS)
        gated = gain_ref[...] * held[which].astype(jnp.float32)
        inner = jnp.sum(gated * values_f, axis=-1, keepdims=True)
        out_ref[...] = (
            row_scale * gated - values_f * (row_scale * row_scale * row_scale * inner / width)
        ).astype(jnp.bfloat16)


def finish(me, queries, keys, gain_q, gain_k, parts):
    rows, width = queries.shape
    part = width // len(parts)
    by_row = pl.BlockSpec((ROW_BLOCK, width), lambda i, me: (i, 0))
    gain = pl.BlockSpec((1, width), lambda i, me: (0, 0))
    return pl.pallas_call(
        finish_kernel,
        grid_spec=pltpu.PrefetchScalarGridSpec(
            num_scalar_prefetch=1,
            grid=(rows // ROW_BLOCK,),
            in_specs=[by_row, by_row, gain, gain]
            + [pl.BlockSpec((3, ROW_BLOCK, part), lambda i, me: (0, i, 0))] * len(parts),
            out_specs=[by_row] * 3,
            scratch_shapes=[pltpu.VMEM((2, ROW_BLOCK, width), jnp.bfloat16)],
        ),
        out_shape=[jax.ShapeDtypeStruct((rows, width), jnp.bfloat16)] * 3,
        compiler_params=pltpu.CompilerParams(vmem_limit_bytes=VMEM_LIMIT),
        name="finish",
    )(me, queries, keys, gain_q[None], gain_k[None], *parts)


def forward_kernel(factor, *refs):
    parts, (bias_ref, probs_ref, out_ref) = refs[:-3], refs[-3:]
    rows = parts[0].shape[1]
    key = jnp.concatenate([part[1] for part in parts], axis=0)
    value_t = jnp.concatenate([part[2] for part in parts], axis=0).T
    for block, part in enumerate(parts):
        at = pl.ds(block * rows, rows)
        scores = dot_nt(key, part[0]) * factor + bias_ref[:, at].astype(jnp.float32)
        weights = jnp.exp(scores - jnp.max(scores, axis=0, keepdims=True))
        probs = weights * (1.0 / jnp.sum(weights, axis=0, keepdims=True))
        probs_low = probs.astype(jnp.bfloat16)
        probs_ref[0, :, at] = probs_low
        out_ref[at, :] = dot_nn(value_t, probs_low).T.astype(jnp.bfloat16)


def backward_kernel(factor, peers, *refs):
    parts, grads, probs_ref = refs[:peers], refs[peers : 2 * peers], refs[2 * peers]
    outs = refs[2 * peers + 1 : 3 * peers + 1]
    dk_sum, dv_sum = refs[3 * peers + 1 :]
    rows = parts[0].shape[1]
    key_t = jnp.concatenate([part[1] for part in parts], axis=0).T
    value = jnp.concatenate([part[2] for part in parts], axis=0)
    for block in range(peers):
        at = pl.ds(block * rows, rows)
        grad = grads[block][...]
        probs_low = probs_ref[0, :, at]
        grad_probs = dot_nt(value, grad)
        probs = probs_low.astype(jnp.float32)
        delta = jnp.sum(probs * grad_probs, axis=0, keepdims=True)
        grad_scores = (probs * (grad_probs - delta)).astype(jnp.bfloat16)
        dv_part = dot_nn(probs_low, grad)
        dk_part = dot_nn(grad_scores, parts[block][0])
        if block == 0:
            dv_sum[...] = dv_part
            dk_sum[...] = dk_part
        else:
            dv_sum[...] += dv_part
            dk_sum[...] += dk_part
        outs[block][0] = (dot_nn(key_t, grad_scores) * factor).T.astype(jnp.bfloat16)
    for block in range(peers):
        at = pl.ds(block * rows, rows)
        outs[block][1] = (dk_sum[at, :] * factor).astype(jnp.bfloat16)
        outs[block][2] = dv_sum[at, :].astype(jnp.bfloat16)


def attention_forward(parts, bias):
    peers = len(parts)
    _, rows, width = parts[0].shape
    heads = width // HEAD_DIM
    total = peers * rows
    pairs = heads * total * total
    return pl.pallas_call(
        functools.partial(forward_kernel, 1.0 / math.sqrt(HEAD_DIM)),
        grid=(heads,),
        in_specs=[pl.BlockSpec((3, rows, HEAD_DIM), lambda h: (0, 0, h))] * peers
        + [pl.BlockSpec((total, total), lambda h: (0, 0))],
        out_specs=[
            pl.BlockSpec((1, total, total), lambda h: (h, 0, 0)),
            pl.BlockSpec((total, HEAD_DIM), lambda h: (0, h)),
        ],
        out_shape=[
            jax.ShapeDtypeStruct((heads, total, total), jnp.bfloat16),
            jax.ShapeDtypeStruct((total, width), jnp.bfloat16),
        ],
        compiler_params=pltpu.CompilerParams(vmem_limit_bytes=VMEM_LIMIT),
        cost_estimate=pl.CostEstimate(
            flops=4 * pairs * HEAD_DIM, bytes_accessed=4 * pairs, transcendentals=pairs
        ),
        name="attention_forward",
    )(*parts, bias)


def attention_backward(parts, grads, probs):
    peers = len(parts)
    _, rows, width = parts[0].shape
    heads = width // HEAD_DIM
    total = peers * rows
    pairs = heads * total * total
    by_part = pl.BlockSpec((3, rows, HEAD_DIM), lambda h: (0, 0, h))
    return pl.pallas_call(
        functools.partial(backward_kernel, 1.0 / math.sqrt(HEAD_DIM), peers),
        grid=(heads,),
        in_specs=[by_part] * peers
        + [pl.BlockSpec((rows, HEAD_DIM), lambda h: (0, h))] * peers
        + [pl.BlockSpec((1, total, total), lambda h: (h, 0, 0))],
        out_specs=[by_part] * peers,
        out_shape=[jax.ShapeDtypeStruct((3, rows, width), jnp.bfloat16)] * peers,
        scratch_shapes=[
            pltpu.VMEM((total, HEAD_DIM), jnp.float32),
            pltpu.VMEM((total, HEAD_DIM), jnp.float32),
        ],
        compiler_params=pltpu.CompilerParams(vmem_limit_bytes=VMEM_LIMIT),
        cost_estimate=pl.CostEstimate(
            flops=8 * pairs * HEAD_DIM, bytes_accessed=4 * pairs, transcendentals=0
        ),
        name="attention_backward",
    )(*parts, *grads, probs)


def weight_kernel(scale, *refs):
    cots, (att_ref, out_ref) = refs[:-2], refs[-2:]
    cot = jnp.concatenate([cot[...] for cot in cots], axis=0)
    out_ref[...] = (dot_tn(cot, att_ref[...]) * scale).astype(jnp.bfloat16)


def weight_partial(cots, attended, scale):
    rows, features = cots[0].shape
    total, width = attended.shape
    block = 512
    return pl.pallas_call(
        functools.partial(weight_kernel, scale),
        grid=(features // block,),
        in_specs=[pl.BlockSpec((rows, block), lambda i: (0, i))] * len(cots)
        + [pl.BlockSpec((total, width), lambda i: (0, 0))],
        out_specs=pl.BlockSpec((block, width), lambda i: (i, 0)),
        out_shape=jax.ShapeDtypeStruct((features, width), jnp.bfloat16),
        compiler_params=pltpu.CompilerParams(vmem_limit_bytes=VMEM_LIMIT),
        cost_estimate=pl.CostEstimate(
            flops=2 * total * features * width,
            bytes_accessed=2 * features * (total + width),
            transcendentals=0,
        ),
        name="weight_partial",
    )(*cots, attended)


def score_bias(tile_pairs, clip_lengths, clip_rows, order):
    tile_count = tile_pairs.shape[0]
    tile_rows = clip_rows // tile_count
    listed = jnp.any(tile_pairs[order][:, :, None] == order[None, None, :], axis=1)
    lengths = jnp.where(listed, clip_lengths[order][None, :], 0)
    live = jnp.arange(tile_rows, dtype=jnp.int32)[None, :, None] < lengths.T[:, None, :]
    bias = jnp.where(live, 0.0, DEAD).astype(jnp.bfloat16).reshape(clip_rows, tile_count)
    return jnp.repeat(bias, tile_rows, axis=1)


def swap(field, step, peers):
    return lax.ppermute(field, "seq", [(i, i ^ step) for i in range(peers)])


def per_device(queries, keys, values, gain_q, gain_k, tile_pairs, tile_lens, out_grad, w_out):
    dp_count = lax.axis_size("dp")
    peers = lax.axis_size("seq")
    position = lax.axis_index("seq")
    me = position.astype(jnp.int32)[None]
    clip_rows = queries.shape[0] * peers
    tile_count = tile_pairs.shape[0]
    near = tile_count // peers
    w_all = lax.all_gather(w_out, "dp", axis=0, tiled=True)
    sends = prepare(me, queries, keys, values, gain_q, gain_k, peers)
    parts = [sends[0]] + [swap(sends[step], step, peers) for step in range(1, peers)]
    cots = [out_grad]
    held = out_grad
    span = 1
    while span < peers:
        if span > 1:
            held = lax.optimization_barrier((out_grad, parts[span:]))[0]
        far = swap(held, span, peers)
        cots += [far] + [swap(far, step, peers) for step in range(1, span)]
        span *= 2
    tiles = jnp.arange(tile_count, dtype=jnp.int32)
    order = ((tiles // near) ^ position) * near + tiles % near
    bias = score_bias(tile_pairs, tile_lens[0], clip_rows, order)
    probs, attended = attention_forward(parts, bias)
    partial_w = weight_partial(cots, attended, 1.0 / dp_count)
    grad_w = lax.psum_scatter(partial_w, "dp", scatter_dimension=0, tiled=True)
    grads = [dot_nn(cot, w_all).astype(jnp.bfloat16) for cot in cots]
    backs = attention_backward(parts, grads, probs)
    backs = [backs[0]] + [swap(backs[step], step, peers) for step in range(1, peers)]
    grad_q, grad_k, grad_v = finish(me, queries, keys, gain_q, gain_k, backs)
    return (grad_q, grad_k, grad_v, grad_w.astype(jnp.float32))


def solution(mesh):
    return jax.shard_map(
        per_device,
        mesh=mesh,
        in_specs=(
            P(("dp", "seq"), None),
            P(("dp", "seq"), None),
            P(("dp", "seq"), None),
            P(),
            P(),
            P(),
            P("dp", None),
            P(("dp", "seq"), None),
            P("dp", "seq"),
        ),
        out_specs=(
            P(("dp", "seq"), None),
            P(("dp", "seq"), None),
            P(("dp", "seq"), None),
            P("dp", "seq"),
        ),
        check_vma=False,
    )
```

```python
import functools
import math

import jax
import jax.numpy as jnp
from jax import lax
from jax.experimental import pallas as pl
from jax.experimental.pallas import tpu as pltpu
from jax.sharding import PartitionSpec as P

HEAD_DIM = 128
ROW_BLOCK = 64
EPS = 1e-06
DEAD = -1e30
VMEM_LIMIT = 48 * 1024 * 1024


def dot_nt(left, right):
    return lax.dot_general(
        left, right, (((1,), (1,)), ((), ())), preferred_element_type=jnp.float32
    )


def dot_tn(left, right):
    return lax.dot_general(
        left, right, (((0,), (0,)), ((), ())), preferred_element_type=jnp.float32
    )


def dot_nn(left, right):
    return jnp.dot(left, right, preferred_element_type=jnp.float32)


def columns_of(owner, width):
    return pl.ds(pl.multiple_of(owner * width, HEAD_DIM), width)


def prepare_kernel(me_ref, q_ref, k_ref, v_ref, gain_q_ref, gain_k_ref, *rest):
    sends, held = rest[:-1], rest[-1]
    for which, (field_ref, gain_ref) in enumerate(((q_ref, gain_q_ref), (k_ref, gain_k_ref))):
        values_f = field_ref[...].astype(jnp.float32)
        row_scale = lax.rsqrt(jnp.mean(values_f * values_f, axis=-1, keepdims=True) + EPS)
        held[which] = (values_f * row_scale * gain_ref[...]).astype(jnp.bfloat16)
    held[2] = v_ref[...]
    for step, send_ref in enumerate(sends):
        part = columns_of(me_ref[0] ^ step, send_ref.shape[2])
        for which in range(3):
            send_ref[which] = held[which, :, part]


def prepare(me, queries, keys, values, gain_q, gain_k, peers):
    rows, width = queries.shape
    part = width // peers
    by_row = pl.BlockSpec((ROW_BLOCK, width), lambda i, me: (i, 0))
    gain = pl.BlockSpec((1, width), lambda i, me: (0, 0))
    return pl.pallas_call(
        prepare_kernel,
        grid_spec=pltpu.PrefetchScalarGridSpec(
            num_scalar_prefetch=1,
            grid=(rows // ROW_BLOCK,),
            in_specs=[by_row, by_row, by_row, gain, gain],
            out_specs=[pl.BlockSpec((3, ROW_BLOCK, part), lambda i, me: (0, i, 0))] * peers,
            scratch_shapes=[pltpu.VMEM((3, ROW_BLOCK, width), jnp.bfloat16)],
        ),
        out_shape=[jax.ShapeDtypeStruct((3, rows, part), jnp.bfloat16)] * peers,
        compiler_params=pltpu.CompilerParams(vmem_limit_bytes=VMEM_LIMIT),
        name="prepare",
    )(me, queries, keys, values, gain_q[None], gain_k[None])


def finish_kernel(me_ref, q_ref, k_ref, gain_q_ref, gain_k_ref, *rest):
    parts, (dq_ref, dk_ref, dv_ref, held) = rest[:-4], rest[-4:]
    for step, part_ref in enumerate(parts):
        part = columns_of(me_ref[0] ^ step, part_ref.shape[2])
        held[0, :, part] = part_ref[0]
        held[1, :, part] = part_ref[1]
        dv_ref[:, part] = part_ref[2]
    for which, (field_ref, gain_ref, out_ref) in enumerate(
        ((q_ref, gain_q_ref, dq_ref), (k_ref, gain_k_ref, dk_ref))
    ):
        values_f = field_ref[...].astype(jnp.float32)
        width = values_f.shape[1]
        row_scale = lax.rsqrt(jnp.mean(values_f * values_f, axis=-1, keepdims=True) + EPS)
        gated = gain_ref[...] * held[which].astype(jnp.float32)
        inner = jnp.sum(gated * values_f, axis=-1, keepdims=True)
        out_ref[...] = (
            row_scale * gated - values_f * (row_scale * row_scale * row_scale * inner / width)
        ).astype(jnp.bfloat16)


def finish(me, queries, keys, gain_q, gain_k, parts):
    rows, width = queries.shape
    part = width // len(parts)
    by_row = pl.BlockSpec((ROW_BLOCK, width), lambda i, me: (i, 0))
    gain = pl.BlockSpec((1, width), lambda i, me: (0, 0))
    return pl.pallas_call(
        finish_kernel,
        grid_spec=pltpu.PrefetchScalarGridSpec(
            num_scalar_prefetch=1,
            grid=(rows // ROW_BLOCK,),
            in_specs=[by_row, by_row, gain, gain]
            + [pl.BlockSpec((3, ROW_BLOCK, part), lambda i, me: (0, i, 0))] * len(parts),
            out_specs=[by_row] * 3,
            scratch_shapes=[pltpu.VMEM((2, ROW_BLOCK, width), jnp.bfloat16)],
        ),
        out_shape=[jax.ShapeDtypeStruct((rows, width), jnp.bfloat16)] * 3,
        compiler_params=pltpu.CompilerParams(vmem_limit_bytes=VMEM_LIMIT),
        name="finish",
    )(me, queries, keys, gain_q[None], gain_k[None], *parts)


def forward_kernel(factor, *refs):
    parts, (bias_ref, probs_ref, out_ref) = refs[:-3], refs[-3:]
    rows = parts[0].shape[1]
    key = jnp.concatenate([part[1] for part in parts], axis=0)
    value_t = jnp.concatenate([part[2] for part in parts], axis=0).T
    for block, part in enumerate(parts):
        at = pl.ds(block * rows, rows)
        scores = dot_nt(key, part[0]) * factor + bias_ref[:, at].astype(jnp.float32)
        weights = jnp.exp(scores - jnp.max(scores, axis=0, keepdims=True))
        probs = weights * (1.0 / jnp.sum(weights, axis=0, keepdims=True))
        probs_low = probs.astype(jnp.bfloat16)
        probs_ref[0, :, at] = probs_low
        out_ref[at, :] = dot_nn(value_t, probs_low).T.astype(jnp.bfloat16)


def backward_kernel(factor, peers, *refs):
    parts, (grad_ref, probs_ref) = refs[:peers], refs[peers : peers + 2]
    outs = refs[peers + 2 : 2 * peers + 2]
    dk_sum, dv_sum = refs[2 * peers + 2 :]
    rows = parts[0].shape[1]
    key_t = jnp.concatenate([part[1] for part in parts], axis=0).T
    value = jnp.concatenate([part[2] for part in parts], axis=0)
    for block in range(peers):
        at = pl.ds(block * rows, rows)
        grad = grad_ref[at, :]
        probs_low = probs_ref[0, :, at]
        grad_probs = dot_nt(value, grad)
        probs = probs_low.astype(jnp.float32)
        delta = jnp.sum(probs * grad_probs, axis=0, keepdims=True)
        grad_scores = (probs * (grad_probs - delta)).astype(jnp.bfloat16)
        dv_part = dot_nn(probs_low, grad)
        dk_part = dot_nn(grad_scores, parts[block][0])
        if block == 0:
            dv_sum[...] = dv_part
            dk_sum[...] = dk_part
        else:
            dv_sum[...] += dv_part
            dk_sum[...] += dk_part
        outs[block][0] = (dot_nn(key_t, grad_scores) * factor).T.astype(jnp.bfloat16)
    for block in range(peers):
        at = pl.ds(block * rows, rows)
        outs[block][1] = (dk_sum[at, :] * factor).astype(jnp.bfloat16)
        outs[block][2] = dv_sum[at, :].astype(jnp.bfloat16)


def attention_forward(parts, bias):
    peers = len(parts)
    _, rows, width = parts[0].shape
    heads = width // HEAD_DIM
    total = peers * rows
    pairs = heads * total * total
    return pl.pallas_call(
        functools.partial(forward_kernel, 1.0 / math.sqrt(HEAD_DIM)),
        grid=(heads,),
        in_specs=[pl.BlockSpec((3, rows, HEAD_DIM), lambda h: (0, 0, h))] * peers
        + [pl.BlockSpec((total, total), lambda h: (0, 0))],
        out_specs=[
            pl.BlockSpec((1, total, total), lambda h: (h, 0, 0)),
            pl.BlockSpec((total, HEAD_DIM), lambda h: (0, h)),
        ],
        out_shape=[
            jax.ShapeDtypeStruct((heads, total, total), jnp.bfloat16),
            jax.ShapeDtypeStruct((total, width), jnp.bfloat16),
        ],
        compiler_params=pltpu.CompilerParams(vmem_limit_bytes=VMEM_LIMIT),
        cost_estimate=pl.CostEstimate(
            flops=4 * pairs * HEAD_DIM, bytes_accessed=4 * pairs, transcendentals=pairs
        ),
        name="attention_forward",
    )(*parts, bias)


def attention_backward(parts, grad, probs):
    peers = len(parts)
    _, rows, width = parts[0].shape
    heads = width // HEAD_DIM
    total = peers * rows
    pairs = heads * total * total
    by_part = pl.BlockSpec((3, rows, HEAD_DIM), lambda h: (0, 0, h))
    return pl.pallas_call(
        functools.partial(backward_kernel, 1.0 / math.sqrt(HEAD_DIM), peers),
        grid=(heads,),
        in_specs=[by_part] * peers
        + [pl.BlockSpec((total, HEAD_DIM), lambda h: (0, h))]
        + [pl.BlockSpec((1, total, total), lambda h: (h, 0, 0))],
        out_specs=[by_part] * peers,
        out_shape=[jax.ShapeDtypeStruct((3, rows, width), jnp.bfloat16)] * peers,
        scratch_shapes=[
            pltpu.VMEM((total, HEAD_DIM), jnp.float32),
            pltpu.VMEM((total, HEAD_DIM), jnp.float32),
        ],
        compiler_params=pltpu.CompilerParams(vmem_limit_bytes=VMEM_LIMIT),
        cost_estimate=pl.CostEstimate(
            flops=8 * pairs * HEAD_DIM, bytes_accessed=4 * pairs, transcendentals=0
        ),
        name="attention_backward",
    )(*parts, grad, probs)


def weight_kernel(scale, *refs):
    cots, (att_ref, out_ref) = refs[:-2], refs[-2:]
    cot = jnp.concatenate([cot[...] for cot in cots], axis=0)
    out_ref[...] = (dot_tn(cot, att_ref[...]) * scale).astype(jnp.bfloat16)


def weight_partial(cots, attended, scale):
    rows, features = cots[0].shape
    total, width = attended.shape
    block = 512
    return pl.pallas_call(
        functools.partial(weight_kernel, scale),
        grid=(features // block,),
        in_specs=[pl.BlockSpec((rows, block), lambda i: (0, i))] * len(cots)
        + [pl.BlockSpec((total, width), lambda i: (0, 0))],
        out_specs=pl.BlockSpec((block, width), lambda i: (i, 0)),
        out_shape=jax.ShapeDtypeStruct((features, width), jnp.bfloat16),
        compiler_params=pltpu.CompilerParams(vmem_limit_bytes=VMEM_LIMIT),
        cost_estimate=pl.CostEstimate(
            flops=2 * total * features * width,
            bytes_accessed=2 * features * (total + width),
            transcendentals=0,
        ),
        name="weight_partial",
    )(*cots, attended)


def project_kernel(peers, *refs):
    firsts, seconds, (w_ref, out_ref, total) = refs[:peers], refs[peers : 2 * peers], refs[2 * peers :]
    step = pl.program_id(0)
    width = w_ref.shape[2]
    first = firsts[0].shape[1] // w_ref.shape[0]
    w_first = w_ref[:, :first, :].reshape(firsts[0].shape[1], width)
    w_second = w_ref[:, first:, :].reshape(seconds[0].shape[1], width)
    product = dot_nn(jnp.concatenate([ref[...] for ref in firsts], axis=0), w_first)
    product += dot_nn(jnp.concatenate([ref[...] for ref in seconds], axis=0), w_second)

    @pl.when(step == 0)
    def _():
        total[...] = product

    @pl.when(step > 0)
    def _():
        total[...] += product

    @pl.when(step == pl.num_programs(0) - 1)
    def _():
        out_ref[...] = total[...].astype(jnp.bfloat16)


def project(firsts, seconds, w_all, group):
    peers = len(firsts)
    rows = firsts[0].shape[0]
    owners, depth, width = w_all.shape
    steps = owners // group
    total = peers * rows
    return pl.pallas_call(
        functools.partial(project_kernel, peers),
        grid=(steps,),
        in_specs=[pl.BlockSpec((rows, firsts[0].shape[1] // steps), lambda i: (0, i))] * peers
        + [pl.BlockSpec((rows, seconds[0].shape[1] // steps), lambda i: (0, i))] * peers
        + [pl.BlockSpec((group, depth, width), lambda i: (i, 0, 0))],
        out_specs=pl.BlockSpec((total, width), lambda i: (0, 0)),
        out_shape=jax.ShapeDtypeStruct((total, width), jnp.bfloat16),
        scratch_shapes=[pltpu.VMEM((total, width), jnp.float32)],
        compiler_params=pltpu.CompilerParams(vmem_limit_bytes=VMEM_LIMIT),
        cost_estimate=pl.CostEstimate(
            flops=2 * total * owners * depth * width,
            bytes_accessed=2 * owners * depth * (total + width),
            transcendentals=0,
        ),
        name="project",
    )(*firsts, *seconds, w_all)


def score_bias(tile_pairs, clip_lengths, clip_rows, order):
    tile_count = tile_pairs.shape[0]
    tile_rows = clip_rows // tile_count
    listed = jnp.any(tile_pairs[order][:, :, None] == order[None, None, :], axis=1)
    lengths = jnp.where(listed, clip_lengths[order][None, :], 0)
    live = jnp.arange(tile_rows, dtype=jnp.int32)[None, :, None] < lengths.T[:, None, :]
    bias = jnp.where(live, 0.0, DEAD).astype(jnp.bfloat16).reshape(clip_rows, tile_count)
    return jnp.repeat(bias, tile_rows, axis=1)


def swap(field, step, peers):
    return lax.ppermute(field, "seq", [(i, i ^ step) for i in range(peers)])


def gather_rows(mine, before, after, peers):
    blocks = [mine]
    span = 1
    far = mine
    while span < peers:
        held = mine if span == 1 else lax.optimization_barrier((mine, before))[0]
        far = swap(held, span, peers)
        blocks.append(far)
        if span > 1:
            handed = lax.optimization_barrier((far, after))[0]
            blocks += [swap(handed, step, peers) for step in range(1, span)]
        span *= 2
    return blocks, far


def pairwise_sum(field, before):
    count = field.shape[0]
    position = lax.axis_index("dp")
    bit = 1
    while bit < count:
        pairs = field.reshape((field.shape[0] // 2, 2) + field.shape[1:])
        side = (position // bit) % 2
        kept = lax.dynamic_index_in_dim(pairs, side, 1, keepdims=False)
        sent = lax.dynamic_index_in_dim(pairs, 1 - side, 1, keepdims=False)
        got = lax.ppermute(sent, "dp", [(i, i ^ bit) for i in range(count)])
        if bit == 1:
            got = lax.optimization_barrier((got, before))[0]
        field = (kept.astype(jnp.float32) + got.astype(jnp.float32)).astype(jnp.bfloat16)
        bit *= 2
    return field[0]


def per_device(queries, keys, values, gain_q, gain_k, tile_pairs, tile_lens, out_grad, w_out):
    dp_count = lax.axis_size("dp")
    peers = lax.axis_size("seq")
    position = lax.axis_index("seq")
    me = position.astype(jnp.int32)[None]
    rows = queries.shape[0]
    clip_rows = rows * peers
    tile_count = tile_pairs.shape[0]
    near = tile_count // peers
    depth, width = w_out.shape
    first = depth * 3 // 5
    group = max(1, 5 * HEAD_DIM // depth)
    w_all = lax.all_gather(w_out, "dp", axis=0, tiled=False)
    sends = prepare(me, queries, keys, values, gain_q, gain_k, peers)
    parts = [sends[0]] + [swap(sends[step], step, peers) for step in range(1, peers)]
    by_owner = out_grad.reshape(rows, dp_count, depth)
    mine_first = by_owner[:, :, :first].reshape(rows, -1)
    mine_second = by_owner[:, :, first:].reshape(rows, -1)
    tiles = jnp.arange(tile_count, dtype=jnp.int32)
    order = ((tiles // near) ^ position) * near + tiles % near
    bias = score_bias(tile_pairs, tile_lens[0], clip_rows, order)
    probs, attended = attention_forward(parts, bias)
    firsts, far_first = gather_rows(mine_first, parts, attended, peers)
    partial_first = weight_partial(firsts, attended, 1.0 / dp_count)
    grad_w_first = lax.psum_scatter(partial_first, "dp", scatter_dimension=0, tiled=True)
    seconds, _ = gather_rows(mine_second, far_first, partial_first, peers)
    partial_second = weight_partial(seconds, attended, 1.0 / dp_count)
    grad = project(firsts, seconds, w_all, group)
    backs = attention_backward(parts, grad, probs)
    grad_w_second = pairwise_sum(partial_second.reshape(dp_count, depth - first, width), backs)
    backs = [backs[0]] + [swap(backs[step], step, peers) for step in range(1, peers)]
    grad_q, grad_k, grad_v = finish(me, queries, keys, gain_q, gain_k, backs)
    grad_w = jnp.concatenate([grad_w_first, grad_w_second], axis=0)
    return (grad_q, grad_k, grad_v, grad_w.astype(jnp.float32))


def solution(mesh):
    return jax.shard_map(
        per_device,
        mesh=mesh,
        in_specs=(
            P(("dp", "seq"), None),
            P(("dp", "seq"), None),
            P(("dp", "seq"), None),
            P(),
            P(),
            P(),
            P("dp", None),
            P(("dp", "seq"), None),
            P("dp", "seq"),
        ),
        out_specs=(
            P(("dp", "seq"), None),
            P(("dp", "seq"), None),
            P(("dp", "seq"), None),
            P("dp", "seq"),
        ),
        check_vma=False,
    )
```

```python
import functools
import math

import jax
import jax.numpy as jnp
from jax import lax
from jax.experimental import pallas as pl
from jax.experimental.pallas import tpu as pltpu
from jax.sharding import PartitionSpec as P

HEAD_DIM = 128
ROW_BLOCK = 64
EPS = 1e-06
DEAD = -1e30
VMEM_LIMIT = 48 * 1024 * 1024


def dot_nt(left, right):
    return lax.dot_general(
        left, right, (((1,), (1,)), ((), ())), preferred_element_type=jnp.float32
    )


def dot_tn(left, right):
    return lax.dot_general(
        left, right, (((0,), (0,)), ((), ())), preferred_element_type=jnp.float32
    )


def dot_nn(left, right):
    return jnp.dot(left, right, preferred_element_type=jnp.float32)


def columns_of(owner, width):
    return pl.ds(pl.multiple_of(owner * width, HEAD_DIM), width)


def prepare_kernel(me_ref, q_ref, k_ref, v_ref, gain_q_ref, gain_k_ref, *rest):
    sends, held = rest[:-1], rest[-1]
    for which, (field_ref, gain_ref) in enumerate(((q_ref, gain_q_ref), (k_ref, gain_k_ref))):
        values_f = field_ref[...].astype(jnp.float32)
        row_scale = lax.rsqrt(jnp.mean(values_f * values_f, axis=-1, keepdims=True) + EPS)
        held[which] = (values_f * row_scale * gain_ref[...]).astype(jnp.bfloat16)
    held[2] = v_ref[...]
    for step, send_ref in enumerate(sends):
        part = columns_of(me_ref[0] ^ step, send_ref.shape[2])
        for which in range(3):
            send_ref[which] = held[which, :, part]


def prepare(me, queries, keys, values, gain_q, gain_k, peers):
    rows, width = queries.shape
    part = width // peers
    by_row = pl.BlockSpec((ROW_BLOCK, width), lambda i, me: (i, 0))
    gain = pl.BlockSpec((1, width), lambda i, me: (0, 0))
    return pl.pallas_call(
        prepare_kernel,
        grid_spec=pltpu.PrefetchScalarGridSpec(
            num_scalar_prefetch=1,
            grid=(rows // ROW_BLOCK,),
            in_specs=[by_row, by_row, by_row, gain, gain],
            out_specs=[pl.BlockSpec((3, ROW_BLOCK, part), lambda i, me: (0, i, 0))] * peers,
            scratch_shapes=[pltpu.VMEM((3, ROW_BLOCK, width), jnp.bfloat16)],
        ),
        out_shape=[jax.ShapeDtypeStruct((3, rows, part), jnp.bfloat16)] * peers,
        compiler_params=pltpu.CompilerParams(vmem_limit_bytes=VMEM_LIMIT),
        name="prepare",
    )(me, queries, keys, values, gain_q[None], gain_k[None])


def finish_kernel(peers, begins, me_ref, q_ref, k_ref, gain_q_ref, gain_k_ref, *rest):
    parts, (dq_ref, dk_ref, dv_ref, held) = rest[:-4], rest[-4:]
    for index, part_ref in enumerate(parts):
        step, begin = index % peers, HEAD_DIM * begins[index // peers]
        start = (me_ref[0] ^ step) * (q_ref.shape[1] // peers) + begin
        part = pl.ds(pl.multiple_of(start, HEAD_DIM), part_ref.shape[2])
        held[0, :, part] = part_ref[0]
        held[1, :, part] = part_ref[1]
        dv_ref[:, part] = part_ref[2]
    for which, (field_ref, gain_ref, out_ref) in enumerate(
        ((q_ref, gain_q_ref, dq_ref), (k_ref, gain_k_ref, dk_ref))
    ):
        values_f = field_ref[...].astype(jnp.float32)
        width = values_f.shape[1]
        row_scale = lax.rsqrt(jnp.mean(values_f * values_f, axis=-1, keepdims=True) + EPS)
        gated = gain_ref[...] * held[which].astype(jnp.float32)
        inner = jnp.sum(gated * values_f, axis=-1, keepdims=True)
        out_ref[...] = (
            row_scale * gated - values_f * (row_scale * row_scale * row_scale * inner / width)
        ).astype(jnp.bfloat16)


def finish(me, queries, keys, gain_q, gain_k, parts, peers, begins):
    rows, width = queries.shape
    by_row = pl.BlockSpec((ROW_BLOCK, width), lambda i, me: (i, 0))
    gain = pl.BlockSpec((1, width), lambda i, me: (0, 0))
    return pl.pallas_call(
        functools.partial(finish_kernel, peers, begins),
        grid_spec=pltpu.PrefetchScalarGridSpec(
            num_scalar_prefetch=1,
            grid=(rows // ROW_BLOCK,),
            in_specs=[by_row, by_row, gain, gain]
            + [
                pl.BlockSpec((3, ROW_BLOCK, part.shape[2]), lambda i, me: (0, i, 0))
                for part in parts
            ],
            out_specs=[by_row] * 3,
            scratch_shapes=[pltpu.VMEM((2, ROW_BLOCK, width), jnp.bfloat16)],
        ),
        out_shape=[jax.ShapeDtypeStruct((rows, width), jnp.bfloat16)] * 3,
        compiler_params=pltpu.CompilerParams(vmem_limit_bytes=VMEM_LIMIT),
        name="finish",
    )(me, queries, keys, gain_q[None], gain_k[None], *parts)


def forward_kernel(factor, *refs):
    parts, (bias_ref, probs_ref, out_ref) = refs[:-3], refs[-3:]
    rows = parts[0].shape[1]
    key = jnp.concatenate([part[1] for part in parts], axis=0)
    value_t = jnp.concatenate([part[2] for part in parts], axis=0).T
    for block, part in enumerate(parts):
        at = pl.ds(block * rows, rows)
        scores = dot_nt(key, part[0]) * factor + bias_ref[:, at].astype(jnp.float32)
        weights = jnp.exp(scores - jnp.max(scores, axis=0, keepdims=True))
        probs = weights * (1.0 / jnp.sum(weights, axis=0, keepdims=True))
        probs_low = probs.astype(jnp.bfloat16)
        probs_ref[0, :, at] = probs_low
        out_ref[at, :] = dot_nn(value_t, probs_low).T.astype(jnp.bfloat16)


def backward_kernel(factor, peers, *refs):
    parts, (grad_ref, probs_ref) = refs[:peers], refs[peers : peers + 2]
    outs = refs[peers + 2 : 2 * peers + 2]
    dk_sum, dv_sum = refs[2 * peers + 2 :]
    rows = parts[0].shape[1]
    key_t = jnp.concatenate([part[1] for part in parts], axis=0).T
    value = jnp.concatenate([part[2] for part in parts], axis=0)
    for block in range(peers):
        at = pl.ds(block * rows, rows)
        grad = grad_ref[at, :]
        probs_low = probs_ref[0, :, at]
        grad_probs = dot_nt(value, grad)
        probs = probs_low.astype(jnp.float32)
        delta = jnp.sum(probs * grad_probs, axis=0, keepdims=True)
        grad_scores = (probs * (grad_probs - delta)).astype(jnp.bfloat16)
        dv_part = dot_nn(probs_low, grad)
        dk_part = dot_nn(grad_scores, parts[block][0])
        if block == 0:
            dv_sum[...] = dv_part
            dk_sum[...] = dk_part
        else:
            dv_sum[...] += dv_part
            dk_sum[...] += dk_part
        outs[block][0] = (dot_nn(key_t, grad_scores) * factor).T.astype(jnp.bfloat16)
    for block in range(peers):
        at = pl.ds(block * rows, rows)
        outs[block][1] = (dk_sum[at, :] * factor).astype(jnp.bfloat16)
        outs[block][2] = dv_sum[at, :].astype(jnp.bfloat16)


def attention_forward(parts, bias):
    peers = len(parts)
    _, rows, width = parts[0].shape
    heads = width // HEAD_DIM
    total = peers * rows
    pairs = heads * total * total
    return pl.pallas_call(
        functools.partial(forward_kernel, 1.0 / math.sqrt(HEAD_DIM)),
        grid=(heads,),
        in_specs=[pl.BlockSpec((3, rows, HEAD_DIM), lambda h: (0, 0, h))] * peers
        + [pl.BlockSpec((total, total), lambda h: (0, 0))],
        out_specs=[
            pl.BlockSpec((1, total, total), lambda h: (h, 0, 0)),
            pl.BlockSpec((total, HEAD_DIM), lambda h: (0, h)),
        ],
        out_shape=[
            jax.ShapeDtypeStruct((heads, total, total), jnp.bfloat16),
            jax.ShapeDtypeStruct((total, width), jnp.bfloat16),
        ],
        compiler_params=pltpu.CompilerParams(vmem_limit_bytes=VMEM_LIMIT),
        cost_estimate=pl.CostEstimate(
            flops=4 * pairs * HEAD_DIM, bytes_accessed=4 * pairs, transcendentals=pairs
        ),
        name="attention_forward",
    )(*parts, bias)


def attention_backward(parts, grad, probs, begin, heads):
    peers = len(parts)
    rows = parts[0].shape[1]
    total = peers * rows
    pairs = heads * total * total
    by_part = pl.BlockSpec((3, rows, HEAD_DIM), lambda h: (0, 0, h + begin))
    return pl.pallas_call(
        functools.partial(backward_kernel, 1.0 / math.sqrt(HEAD_DIM), peers),
        grid=(heads,),
        in_specs=[by_part] * peers
        + [pl.BlockSpec((total, HEAD_DIM), lambda h: (0, h + begin))]
        + [pl.BlockSpec((1, total, total), lambda h: (h + begin, 0, 0))],
        out_specs=[pl.BlockSpec((3, rows, HEAD_DIM), lambda h: (0, 0, h))] * peers,
        out_shape=[jax.ShapeDtypeStruct((3, rows, heads * HEAD_DIM), jnp.bfloat16)] * peers,
        scratch_shapes=[
            pltpu.VMEM((total, HEAD_DIM), jnp.float32),
            pltpu.VMEM((total, HEAD_DIM), jnp.float32),
        ],
        compiler_params=pltpu.CompilerParams(vmem_limit_bytes=VMEM_LIMIT),
        cost_estimate=pl.CostEstimate(
            flops=8 * pairs * HEAD_DIM, bytes_accessed=4 * pairs, transcendentals=0
        ),
        name="attention_backward",
    )(*parts, grad, probs)


def weight_kernel(scale, *refs):
    cots, (att_ref, out_ref) = refs[:-2], refs[-2:]
    cot = jnp.concatenate([cot[...] for cot in cots], axis=0)
    out_ref[...] = (dot_tn(cot, att_ref[...]) * scale).astype(jnp.bfloat16)


def weight_partial(cots, attended, scale):
    rows, features = cots[0].shape
    total, width = attended.shape
    block = 512
    return pl.pallas_call(
        functools.partial(weight_kernel, scale),
        grid=(features // block,),
        in_specs=[pl.BlockSpec((rows, block), lambda i: (0, i))] * len(cots)
        + [pl.BlockSpec((total, width), lambda i: (0, 0))],
        out_specs=pl.BlockSpec((block, width), lambda i: (i, 0)),
        out_shape=jax.ShapeDtypeStruct((features, width), jnp.bfloat16),
        compiler_params=pltpu.CompilerParams(vmem_limit_bytes=VMEM_LIMIT),
        cost_estimate=pl.CostEstimate(
            flops=2 * total * features * width,
            bytes_accessed=2 * features * (total + width),
            transcendentals=0,
        ),
        name="weight_partial",
    )(*cots, attended)


def project_kernel(peers, begin, *refs):
    cots, w_ref, so_far, (out_ref, total) = refs[:peers], refs[peers], refs[peers + 1 : -2], refs[-2:]
    step = pl.program_id(0)
    wide = cots[0].shape[1]
    depth = wide // w_ref.shape[0]
    weights = w_ref[:, begin : begin + depth, :].reshape(wide, w_ref.shape[2])
    product = dot_nn(jnp.concatenate([ref[...] for ref in cots], axis=0), weights)

    @pl.when(step == 0)
    def _():
        total[...] = product + so_far[0][...] if so_far else product

    @pl.when(step > 0)
    def _():
        total[...] += product

    @pl.when(step == pl.num_programs(0) - 1)
    def _():
        out_ref[...] = total[...].astype(out_ref.dtype)


def project(cots, w_all, begin, group, so_far, dtype):
    peers = len(cots)
    rows, features = cots[0].shape
    owners, depth, width = w_all.shape
    steps = owners // group
    total = peers * rows
    whole = pl.BlockSpec((total, width), lambda i: (0, 0))
    return pl.pallas_call(
        functools.partial(project_kernel, peers, begin),
        grid=(steps,),
        in_specs=[pl.BlockSpec((rows, features // steps), lambda i: (0, i))] * peers
        + [pl.BlockSpec((group, depth, width), lambda i: (i, 0, 0))]
        + [whole] * len(so_far),
        out_specs=whole,
        out_shape=jax.ShapeDtypeStruct((total, width), dtype),
        scratch_shapes=[pltpu.VMEM((total, width), jnp.float32)],
        compiler_params=pltpu.CompilerParams(vmem_limit_bytes=VMEM_LIMIT),
        cost_estimate=pl.CostEstimate(
            flops=2 * total * features * width,
            bytes_accessed=2 * features * total + 2 * owners * depth * width,
            transcendentals=0,
        ),
        name="project",
    )(*cots, w_all, *so_far)


def score_bias(tile_pairs, clip_lengths, clip_rows, order):
    tile_count = tile_pairs.shape[0]
    tile_rows = clip_rows // tile_count
    listed = jnp.any(tile_pairs[order][:, :, None] == order[None, None, :], axis=1)
    lengths = jnp.where(listed, clip_lengths[order][None, :], 0)
    live = jnp.arange(tile_rows, dtype=jnp.int32)[None, :, None] < lengths.T[:, None, :]
    bias = jnp.where(live, 0.0, DEAD).astype(jnp.bfloat16).reshape(clip_rows, tile_count)
    return jnp.repeat(bias, tile_rows, axis=1)


def swap(field, step, peers):
    return lax.ppermute(field, "seq", [(i, i ^ step) for i in range(peers)])


def gather_rows(mine, before, after, peers):
    blocks = [mine]
    span = 1
    far = mine
    while span < peers:
        held = mine if span == 1 else lax.optimization_barrier((mine, before))[0]
        far = swap(held, span, peers)
        blocks.append(far)
        if span > 1:
            handed = lax.optimization_barrier((far, after))[0]
            blocks += [swap(handed, step, peers) for step in range(1, span)]
        span *= 2
    return blocks, far


def pairwise_sum(field, before):
    count = field.shape[0]
    position = lax.axis_index("dp")
    bit = 1
    while bit < count:
        pairs = field.reshape((field.shape[0] // 2, 2) + field.shape[1:])
        side = (position // bit) % 2
        kept = lax.dynamic_index_in_dim(pairs, side, 1, keepdims=False)
        sent = lax.dynamic_index_in_dim(pairs, 1 - side, 1, keepdims=False)
        got = lax.ppermute(sent, "dp", [(i, i ^ bit) for i in range(count)])
        if bit == 1:
            got = lax.optimization_barrier((got, before))[0]
        field = (kept.astype(jnp.float32) + got.astype(jnp.float32)).astype(jnp.bfloat16)
        bit *= 2
    return field[0]


def per_device(queries, keys, values, gain_q, gain_k, tile_pairs, tile_lens, out_grad, w_out):
    dp_count = lax.axis_size("dp")
    peers = lax.axis_size("seq")
    position = lax.axis_index("seq")
    me = position.astype(jnp.int32)[None]
    rows = queries.shape[0]
    clip_rows = rows * peers
    tile_count = tile_pairs.shape[0]
    near = tile_count // peers
    depth, width = w_out.shape
    first = depth * 3 // 5
    group = max(1, 5 * HEAD_DIM // depth)
    w_all = lax.all_gather(w_out, "dp", axis=0, tiled=False)
    sends = prepare(me, queries, keys, values, gain_q, gain_k, peers)
    parts = [sends[0]] + [swap(sends[step], step, peers) for step in range(1, peers)]
    by_owner = out_grad.reshape(rows, dp_count, depth)
    mine_first = by_owner[:, :, :first].reshape(rows, -1)
    mine_second = by_owner[:, :, first:].reshape(rows, -1)
    tiles = jnp.arange(tile_count, dtype=jnp.int32)
    order = ((tiles // near) ^ position) * near + tiles % near
    bias = score_bias(tile_pairs, tile_lens[0], clip_rows, order)
    probs, attended = attention_forward(parts, bias)
    firsts, far_first = gather_rows(mine_first, parts, attended, peers)
    partial_first = weight_partial(firsts, attended, 1.0 / dp_count)
    grad_w_first = lax.psum_scatter(partial_first, "dp", scatter_dimension=0, tiled=True)
    grad_first = project(firsts, w_all, 0, group, [], jnp.float32)
    seconds, _ = gather_rows(mine_second, far_first, (partial_first, grad_first), peers)
    partial_second = weight_partial(seconds, attended, 1.0 / dp_count)
    grad = project(seconds, w_all, first, group, [grad_first], jnp.bfloat16)
    heads = width // HEAD_DIM
    cuts = (0, 1, (heads + 1) // 2, heads)
    backs = []
    for begin, end in zip(cuts, cuts[1:]):
        outs = attention_backward(parts, grad, probs, begin, end - begin)
        backs += [outs[0]] + [swap(outs[step], step, peers) for step in range(1, peers)]
        grad = lax.optimization_barrier((grad, outs, backs[:-peers]))[0]
    grad_w_second = pairwise_sum(partial_second.reshape(dp_count, depth - first, width), outs)
    grad_q, grad_k, grad_v = finish(
        me, queries, keys, gain_q, gain_k, backs, peers, cuts[:-1]
    )
    grad_w = jnp.concatenate([grad_w_first, grad_w_second], axis=0)
    return (grad_q, grad_k, grad_v, grad_w.astype(jnp.float32))


def solution(mesh):
    return jax.shard_map(
        per_device,
        mesh=mesh,
        in_specs=(
            P(("dp", "seq"), None),
            P(("dp", "seq"), None),
            P(("dp", "seq"), None),
            P(),
            P(),
            P(),
            P("dp", None),
            P(("dp", "seq"), None),
            P("dp", "seq"),
        ),
        out_specs=(
            P(("dp", "seq"), None),
            P(("dp", "seq"), None),
            P(("dp", "seq"), None),
            P("dp", "seq"),
        ),
        check_vma=False,
    )
```

```python
import functools
import math

import jax
import jax.numpy as jnp
from jax import lax
from jax.experimental import pallas as pl
from jax.experimental.pallas import tpu as pltpu
from jax.sharding import PartitionSpec as P

HEAD_DIM = 128
ROW_BLOCK = 64
EPS = 1e-06
DEAD = -1e30
VMEM_LIMIT = 48 * 1024 * 1024


def dot_nt(left, right):
    return lax.dot_general(
        left, right, (((1,), (1,)), ((), ())), preferred_element_type=jnp.float32
    )


def dot_tn(left, right):
    return lax.dot_general(
        left, right, (((0,), (0,)), ((), ())), preferred_element_type=jnp.float32
    )


def dot_nn(left, right):
    return jnp.dot(left, right, preferred_element_type=jnp.float32)


def columns_of(owner, width):
    return pl.ds(pl.multiple_of(owner * width, HEAD_DIM), width)


def prepare_kernel(me_ref, q_ref, k_ref, v_ref, gain_q_ref, gain_k_ref, *rest):
    sends, held = rest[:-1], rest[-1]
    for which, (field_ref, gain_ref) in enumerate(((q_ref, gain_q_ref), (k_ref, gain_k_ref))):
        values_f = field_ref[...].astype(jnp.float32)
        row_scale = lax.rsqrt(jnp.mean(values_f * values_f, axis=-1, keepdims=True) + EPS)
        held[which] = (values_f * row_scale * gain_ref[...]).astype(jnp.bfloat16)
    held[2] = v_ref[...]
    for step, send_ref in enumerate(sends):
        part = columns_of(me_ref[0] ^ step, send_ref.shape[2])
        for which in range(3):
            send_ref[which] = held[which, :, part]


def prepare(me, queries, keys, values, gain_q, gain_k, peers):
    rows, width = queries.shape
    part = width // peers
    by_row = pl.BlockSpec((ROW_BLOCK, width), lambda i, me: (i, 0))
    gain = pl.BlockSpec((1, width), lambda i, me: (0, 0))
    return pl.pallas_call(
        prepare_kernel,
        grid_spec=pltpu.PrefetchScalarGridSpec(
            num_scalar_prefetch=1,
            grid=(rows // ROW_BLOCK,),
            in_specs=[by_row, by_row, by_row, gain, gain],
            out_specs=[pl.BlockSpec((3, ROW_BLOCK, part), lambda i, me: (0, i, 0))] * peers,
            scratch_shapes=[pltpu.VMEM((3, ROW_BLOCK, width), jnp.bfloat16)],
        ),
        out_shape=[jax.ShapeDtypeStruct((3, rows, part), jnp.bfloat16)] * peers,
        compiler_params=pltpu.CompilerParams(vmem_limit_bytes=VMEM_LIMIT),
        name="prepare",
    )(me, queries, keys, values, gain_q[None], gain_k[None])


def finish_kernel(me_ref, q_ref, k_ref, gain_q_ref, gain_k_ref, *rest):
    parts, (dq_ref, dk_ref, dv_ref, held) = rest[:-4], rest[-4:]
    for step, part_ref in enumerate(parts):
        part = columns_of(me_ref[0] ^ step, part_ref.shape[2])
        held[0, :, part] = part_ref[0]
        held[1, :, part] = part_ref[1]
        dv_ref[:, part] = part_ref[2]
    for which, (field_ref, gain_ref, out_ref) in enumerate(
        ((q_ref, gain_q_ref, dq_ref), (k_ref, gain_k_ref, dk_ref))
    ):
        values_f = field_ref[...].astype(jnp.float32)
        width = values_f.shape[1]
        row_scale = lax.rsqrt(jnp.mean(values_f * values_f, axis=-1, keepdims=True) + EPS)
        gated = gain_ref[...] * held[which].astype(jnp.float32)
        inner = jnp.sum(gated * values_f, axis=-1, keepdims=True)
        out_ref[...] = (
            row_scale * gated - values_f * (row_scale * row_scale * row_scale * inner / width)
        ).astype(jnp.bfloat16)


def finish(me, queries, keys, gain_q, gain_k, parts):
    rows, width = queries.shape
    part = width // len(parts)
    by_row = pl.BlockSpec((ROW_BLOCK, width), lambda i, me: (i, 0))
    gain = pl.BlockSpec((1, width), lambda i, me: (0, 0))
    return pl.pallas_call(
        finish_kernel,
        grid_spec=pltpu.PrefetchScalarGridSpec(
            num_scalar_prefetch=1,
            grid=(rows // ROW_BLOCK,),
            in_specs=[by_row, by_row, gain, gain]
            + [pl.BlockSpec((3, ROW_BLOCK, part), lambda i, me: (0, i, 0))] * len(parts),
            out_specs=[by_row] * 3,
            scratch_shapes=[pltpu.VMEM((2, ROW_BLOCK, width), jnp.bfloat16)],
        ),
        out_shape=[jax.ShapeDtypeStruct((rows, width), jnp.bfloat16)] * 3,
        compiler_params=pltpu.CompilerParams(vmem_limit_bytes=VMEM_LIMIT),
        name="finish",
    )(me, queries, keys, gain_q[None], gain_k[None], *parts)


def forward_kernel(factor, *refs):
    parts, (bias_ref, probs_ref, out_ref) = refs[:-3], refs[-3:]
    rows = parts[0].shape[1]
    key = jnp.concatenate([part[1] for part in parts], axis=0)
    value_t = jnp.concatenate([part[2] for part in parts], axis=0).T
    for block, part in enumerate(parts):
        at = pl.ds(block * rows, rows)
        scores = dot_nt(key, part[0]) * factor + bias_ref[:, at].astype(jnp.float32)
        weights = jnp.exp(scores - jnp.max(scores, axis=0, keepdims=True))
        probs = weights * (1.0 / jnp.sum(weights, axis=0, keepdims=True))
        probs_low = probs.astype(jnp.bfloat16)
        probs_ref[0, :, at] = probs_low
        out_ref[at, :] = dot_nn(value_t, probs_low).T.astype(jnp.bfloat16)


def backward_kernel(factor, peers, *refs):
    parts, (grad_ref, probs_ref) = refs[:peers], refs[peers : peers + 2]
    outs = refs[peers + 2 : 2 * peers + 2]
    dk_sum, dv_sum = refs[2 * peers + 2 :]
    rows = parts[0].shape[1]
    key_t = jnp.concatenate([part[1] for part in parts], axis=0).T
    value = jnp.concatenate([part[2] for part in parts], axis=0)
    for block in range(peers):
        at = pl.ds(block * rows, rows)
        grad = grad_ref[at, :]
        probs_low = probs_ref[0, :, at]
        grad_probs = dot_nt(value, grad)
        probs = probs_low.astype(jnp.float32)
        delta = jnp.sum(probs * grad_probs, axis=0, keepdims=True)
        grad_scores = (probs * (grad_probs - delta)).astype(jnp.bfloat16)
        dv_part = dot_nn(probs_low, grad)
        dk_part = dot_nn(grad_scores, parts[block][0])
        if block == 0:
            dv_sum[...] = dv_part
            dk_sum[...] = dk_part
        else:
            dv_sum[...] += dv_part
            dk_sum[...] += dk_part
        outs[block][0] = (dot_nn(key_t, grad_scores) * factor).T.astype(jnp.bfloat16)
    for block in range(peers):
        at = pl.ds(block * rows, rows)
        outs[block][1] = (dk_sum[at, :] * factor).astype(jnp.bfloat16)
        outs[block][2] = dv_sum[at, :].astype(jnp.bfloat16)


def attention_forward(parts, bias):
    peers = len(parts)
    _, rows, width = parts[0].shape
    heads = width // HEAD_DIM
    total = peers * rows
    pairs = heads * total * total
    return pl.pallas_call(
        functools.partial(forward_kernel, 1.0 / math.sqrt(HEAD_DIM)),
        grid=(heads,),
        in_specs=[pl.BlockSpec((3, rows, HEAD_DIM), lambda h: (0, 0, h))] * peers
        + [pl.BlockSpec((total, total), lambda h: (0, 0))],
        out_specs=[
            pl.BlockSpec((1, total, total), lambda h: (h, 0, 0)),
            pl.BlockSpec((total, HEAD_DIM), lambda h: (0, h)),
        ],
        out_shape=[
            jax.ShapeDtypeStruct((heads, total, total), jnp.bfloat16),
            jax.ShapeDtypeStruct((total, width), jnp.bfloat16),
        ],
        compiler_params=pltpu.CompilerParams(vmem_limit_bytes=VMEM_LIMIT),
        cost_estimate=pl.CostEstimate(
            flops=4 * pairs * HEAD_DIM, bytes_accessed=4 * pairs, transcendentals=pairs
        ),
        name="attention_forward",
    )(*parts, bias)


def attention_backward(parts, grad, probs):
    peers = len(parts)
    _, rows, width = parts[0].shape
    heads = width // HEAD_DIM
    total = peers * rows
    pairs = heads * total * total
    by_part = pl.BlockSpec((3, rows, HEAD_DIM), lambda h: (0, 0, h))
    return pl.pallas_call(
        functools.partial(backward_kernel, 1.0 / math.sqrt(HEAD_DIM), peers),
        grid=(heads,),
        in_specs=[by_part] * peers
        + [pl.BlockSpec((total, HEAD_DIM), lambda h: (0, h))]
        + [pl.BlockSpec((1, total, total), lambda h: (h, 0, 0))],
        out_specs=[by_part] * peers,
        out_shape=[jax.ShapeDtypeStruct((3, rows, width), jnp.bfloat16)] * peers,
        scratch_shapes=[
            pltpu.VMEM((total, HEAD_DIM), jnp.float32),
            pltpu.VMEM((total, HEAD_DIM), jnp.float32),
        ],
        compiler_params=pltpu.CompilerParams(vmem_limit_bytes=VMEM_LIMIT),
        cost_estimate=pl.CostEstimate(
            flops=8 * pairs * HEAD_DIM, bytes_accessed=4 * pairs, transcendentals=0
        ),
        name="attention_backward",
    )(*parts, grad, probs)


def weight_kernel(scale, *refs):
    cots, (att_ref, out_ref) = refs[:-2], refs[-2:]
    cot = jnp.concatenate([cot[...] for cot in cots], axis=0)
    out_ref[...] = (dot_tn(cot, att_ref[...]) * scale).astype(jnp.bfloat16)


def weight_partial(cots, attended, scale):
    rows, features = cots[0].shape
    total, width = attended.shape
    block = 512
    return pl.pallas_call(
        functools.partial(weight_kernel, scale),
        grid=(features // block,),
        in_specs=[pl.BlockSpec((rows, block), lambda i: (0, i))] * len(cots)
        + [pl.BlockSpec((total, width), lambda i: (0, 0))],
        out_specs=pl.BlockSpec((block, width), lambda i: (i, 0)),
        out_shape=jax.ShapeDtypeStruct((features, width), jnp.bfloat16),
        compiler_params=pltpu.CompilerParams(vmem_limit_bytes=VMEM_LIMIT),
        cost_estimate=pl.CostEstimate(
            flops=2 * total * features * width,
            bytes_accessed=2 * features * (total + width),
            transcendentals=0,
        ),
        name="weight_partial",
    )(*cots, attended)


def project_kernel(peers, *refs):
    firsts, seconds, (w_ref, out_ref, total) = refs[:peers], refs[peers : 2 * peers], refs[2 * peers :]
    step = pl.program_id(0)
    width = w_ref.shape[2]
    first = firsts[0].shape[1] // w_ref.shape[0]
    w_first = w_ref[:, :first, :].reshape(firsts[0].shape[1], width)
    w_second = w_ref[:, first:, :].reshape(seconds[0].shape[1], width)
    product = dot_nn(jnp.concatenate([ref[...] for ref in firsts], axis=0), w_first)
    product += dot_nn(jnp.concatenate([ref[...] for ref in seconds], axis=0), w_second)

    @pl.when(step == 0)
    def _():
        total[...] = product

    @pl.when(step > 0)
    def _():
        total[...] += product

    @pl.when(step == pl.num_programs(0) - 1)
    def _():
        out_ref[...] = total[...].astype(jnp.bfloat16)


def project(firsts, seconds, w_all, group):
    peers = len(firsts)
    rows = firsts[0].shape[0]
    owners, depth, width = w_all.shape
    steps = owners // group
    total = peers * rows
    return pl.pallas_call(
        functools.partial(project_kernel, peers),
        grid=(steps,),
        in_specs=[pl.BlockSpec((rows, firsts[0].shape[1] // steps), lambda i: (0, i))] * peers
        + [pl.BlockSpec((rows, seconds[0].shape[1] // steps), lambda i: (0, i))] * peers
        + [pl.BlockSpec((group, depth, width), lambda i: (i, 0, 0))],
        out_specs=pl.BlockSpec((total, width), lambda i: (0, 0)),
        out_shape=jax.ShapeDtypeStruct((total, width), jnp.bfloat16),
        scratch_shapes=[pltpu.VMEM((total, width), jnp.float32)],
        compiler_params=pltpu.CompilerParams(vmem_limit_bytes=VMEM_LIMIT),
        cost_estimate=pl.CostEstimate(
            flops=2 * total * owners * depth * width,
            bytes_accessed=2 * owners * depth * (total + width),
            transcendentals=0,
        ),
        name="project",
    )(*firsts, *seconds, w_all)


def score_bias(tile_pairs, clip_lengths, clip_rows, order):
    tile_count = tile_pairs.shape[0]
    tile_rows = clip_rows // tile_count
    listed = jnp.any(tile_pairs[order][:, :, None] == order[None, None, :], axis=1)
    lengths = jnp.where(listed, clip_lengths[order][None, :], 0)
    live = jnp.arange(tile_rows, dtype=jnp.int32)[None, :, None] < lengths.T[:, None, :]
    bias = jnp.where(live, 0.0, DEAD).astype(jnp.bfloat16).reshape(clip_rows, tile_count)
    return jnp.repeat(bias, tile_rows, axis=1)


def swap(field, step, peers):
    return lax.ppermute(field, "seq", [(i, i ^ step) for i in range(peers)])


def gather_rows(mine, before, after, peers):
    blocks = [mine]
    span = 1
    far = mine
    while span < peers:
        held = mine if span == 1 else lax.optimization_barrier((mine, before))[0]
        far = swap(held, span, peers)
        blocks.append(far)
        if span > 1:
            handed = lax.optimization_barrier((far, after))[0]
            blocks += [swap(handed, step, peers) for step in range(1, span)]
        span *= 2
    return blocks, far


def pairwise_sum(field, before):
    count = field.shape[0]
    position = lax.axis_index("dp")

    def swapped(sent, step):
        return lax.ppermute(sent, "dp", [(i, i ^ step) for i in range(count)])

    def summed(terms):
        return sum(term.astype(jnp.float32) for term in terms).astype(jnp.bfloat16)

    bit = 1
    while field.shape[0] > 4:
        pairs = field.reshape((field.shape[0] // 2, 2) + field.shape[1:])
        side = (position // bit) % 2
        kept = lax.dynamic_index_in_dim(pairs, side, 1, keepdims=False)
        sent = lax.dynamic_index_in_dim(pairs, 1 - side, 1, keepdims=False)
        got = swapped(sent, bit)
        if bit == 1:
            got = lax.optimization_barrier((got, before))[0]
        field = summed((kept, got))
        bit *= 2
    mine = position // bit
    terms = [lax.dynamic_index_in_dim(field, mine, 0, keepdims=False)]
    for step in range(1, field.shape[0]):
        sent = lax.dynamic_index_in_dim(field, mine ^ step, 0, keepdims=False)
        terms.append(swapped(sent, step * bit))
    return summed(terms)


def per_device(queries, keys, values, gain_q, gain_k, tile_pairs, tile_lens, out_grad, w_out):
    dp_count = lax.axis_size("dp")
    peers = lax.axis_size("seq")
    position = lax.axis_index("seq")
    me = position.astype(jnp.int32)[None]
    rows = queries.shape[0]
    clip_rows = rows * peers
    tile_count = tile_pairs.shape[0]
    near = tile_count // peers
    depth, width = w_out.shape
    first = depth * 3 // 5
    group = 10 * HEAD_DIM // depth
    w_all = lax.all_gather(w_out, "dp", axis=0, tiled=False)
    sends = prepare(me, queries, keys, values, gain_q, gain_k, peers)
    parts = [sends[0]] + [swap(sends[step], step, peers) for step in range(1, peers)]
    by_owner = out_grad.reshape(rows, dp_count, depth)
    mine_first = by_owner[:, :, :first].reshape(rows, -1)
    mine_second = by_owner[:, :, first:].reshape(rows, -1)
    tiles = jnp.arange(tile_count, dtype=jnp.int32)
    order = ((tiles // near) ^ position) * near + tiles % near
    bias = score_bias(tile_pairs, tile_lens[0], clip_rows, order)
    probs, attended = attention_forward(parts, bias)
    firsts, far_first = gather_rows(mine_first, parts, attended, peers)
    partial_first = weight_partial(firsts, attended, 1.0 / dp_count)
    seconds, far_second = gather_rows(mine_second, far_first, partial_first, peers)
    partial_first = lax.optimization_barrier((partial_first, far_second))[0]
    grad_w_first = lax.psum_scatter(partial_first, "dp", scatter_dimension=0, tiled=True)
    partial_second = weight_partial(seconds, attended, 1.0 / dp_count)
    grad = project(firsts, seconds, w_all, group)
    backs = attention_backward(parts, grad, probs)
    grad_w_second = pairwise_sum(partial_second.reshape(dp_count, depth - first, width), backs)
    backs = [backs[0]] + [swap(backs[step], step, peers) for step in range(1, peers)]
    grad_q, grad_k, grad_v = finish(me, queries, keys, gain_q, gain_k, backs)
    grad_w = jnp.concatenate([grad_w_first, grad_w_second], axis=0)
    return (grad_q, grad_k, grad_v, grad_w.astype(jnp.float32))


def solution(mesh):
    return jax.shard_map(
        per_device,
        mesh=mesh,
        in_specs=(
            P(("dp", "seq"), None),
            P(("dp", "seq"), None),
            P(("dp", "seq"), None),
            P(),
            P(),
            P(),
            P("dp", None),
            P(("dp", "seq"), None),
            P("dp", "seq"),
        ),
        out_specs=(
            P(("dp", "seq"), None),
            P(("dp", "seq"), None),
            P(("dp", "seq"), None),
            P("dp", "seq"),
        ),
        check_vma=False,
    )
```

```python
import functools
import math

import jax
import jax.numpy as jnp
from jax import lax
from jax.experimental import pallas as pl
from jax.experimental.pallas import tpu as pltpu
from jax.sharding import PartitionSpec as P

HEAD_DIM = 128
ROW_BLOCK = 64
EPS = 1e-06
DEAD = -1e30
VMEM_LIMIT = 48 * 1024 * 1024


def dot_nt(left, right):
    return lax.dot_general(
        left, right, (((1,), (1,)), ((), ())), preferred_element_type=jnp.float32
    )


def dot_tn(left, right):
    return lax.dot_general(
        left, right, (((0,), (0,)), ((), ())), preferred_element_type=jnp.float32
    )


def dot_nn(left, right):
    return jnp.dot(left, right, preferred_element_type=jnp.float32)


def columns_of(owner, width):
    return pl.ds(pl.multiple_of(owner * width, HEAD_DIM), width)


def prepare_kernel(me_ref, q_ref, k_ref, v_ref, gain_q_ref, gain_k_ref, *rest):
    sends, held = rest[:-1], rest[-1]
    for which, (field_ref, gain_ref) in enumerate(((q_ref, gain_q_ref), (k_ref, gain_k_ref))):
        values_f = field_ref[...].astype(jnp.float32)
        row_scale = lax.rsqrt(jnp.mean(values_f * values_f, axis=-1, keepdims=True) + EPS)
        held[which] = (values_f * row_scale * gain_ref[...]).astype(jnp.bfloat16)
    held[2] = v_ref[...]
    for step, send_ref in enumerate(sends):
        part = columns_of(me_ref[0] ^ step, send_ref.shape[2])
        for which in range(3):
            send_ref[which] = held[which, :, part]


def prepare(me, queries, keys, values, gain_q, gain_k, peers):
    rows, width = queries.shape
    part = width // peers
    by_row = pl.BlockSpec((ROW_BLOCK, width), lambda i, me: (i, 0))
    gain = pl.BlockSpec((1, width), lambda i, me: (0, 0))
    return pl.pallas_call(
        prepare_kernel,
        grid_spec=pltpu.PrefetchScalarGridSpec(
            num_scalar_prefetch=1,
            grid=(rows // ROW_BLOCK,),
            in_specs=[by_row, by_row, by_row, gain, gain],
            out_specs=[pl.BlockSpec((3, ROW_BLOCK, part), lambda i, me: (0, i, 0))] * peers,
            scratch_shapes=[pltpu.VMEM((3, ROW_BLOCK, width), jnp.bfloat16)],
        ),
        out_shape=[jax.ShapeDtypeStruct((3, rows, part), jnp.bfloat16)] * peers,
        compiler_params=pltpu.CompilerParams(vmem_limit_bytes=VMEM_LIMIT),
        name="prepare",
    )(me, queries, keys, values, gain_q[None], gain_k[None])


def finish_kernel(me_ref, q_ref, k_ref, gain_q_ref, gain_k_ref, *rest):
    parts, (dq_ref, dk_ref, dv_ref, held) = rest[:-4], rest[-4:]
    for step, part_ref in enumerate(parts):
        part = columns_of(me_ref[0] ^ step, part_ref.shape[2])
        held[0, :, part] = part_ref[0]
        held[1, :, part] = part_ref[1]
        dv_ref[:, part] = part_ref[2]
    for which, (field_ref, gain_ref, out_ref) in enumerate(
        ((q_ref, gain_q_ref, dq_ref), (k_ref, gain_k_ref, dk_ref))
    ):
        values_f = field_ref[...].astype(jnp.float32)
        width = values_f.shape[1]
        row_scale = lax.rsqrt(jnp.mean(values_f * values_f, axis=-1, keepdims=True) + EPS)
        gated = gain_ref[...] * held[which].astype(jnp.float32)
        inner = jnp.sum(gated * values_f, axis=-1, keepdims=True)
        out_ref[...] = (
            row_scale * gated - values_f * (row_scale * row_scale * row_scale * inner / width)
        ).astype(jnp.bfloat16)


def finish(me, queries, keys, gain_q, gain_k, parts):
    rows, width = queries.shape
    part = width // len(parts)
    by_row = pl.BlockSpec((ROW_BLOCK, width), lambda i, me: (i, 0))
    gain = pl.BlockSpec((1, width), lambda i, me: (0, 0))
    return pl.pallas_call(
        finish_kernel,
        grid_spec=pltpu.PrefetchScalarGridSpec(
            num_scalar_prefetch=1,
            grid=(rows // ROW_BLOCK,),
            in_specs=[by_row, by_row, gain, gain]
            + [pl.BlockSpec((3, ROW_BLOCK, part), lambda i, me: (0, i, 0))] * len(parts),
            out_specs=[by_row] * 3,
            scratch_shapes=[pltpu.VMEM((2, ROW_BLOCK, width), jnp.bfloat16)],
        ),
        out_shape=[jax.ShapeDtypeStruct((rows, width), jnp.bfloat16)] * 3,
        compiler_params=pltpu.CompilerParams(vmem_limit_bytes=VMEM_LIMIT),
        name="finish",
    )(me, queries, keys, gain_q[None], gain_k[None], *parts)


def forward_kernel(factor, *refs):
    parts, (bias_ref, probs_ref, out_ref) = refs[:-3], refs[-3:]
    rows = parts[0].shape[1]
    key = jnp.concatenate([part[1] for part in parts], axis=0)
    value_t = jnp.concatenate([part[2] for part in parts], axis=0).T
    for block, part in enumerate(parts):
        at = pl.ds(block * rows, rows)
        scores = dot_nt(key, part[0]) * factor + bias_ref[:, at].astype(jnp.float32)
        weights = jnp.exp(scores - jnp.max(scores, axis=0, keepdims=True))
        probs = weights * (1.0 / jnp.sum(weights, axis=0, keepdims=True))
        probs_low = probs.astype(jnp.bfloat16)
        probs_ref[0, :, at] = probs_low
        out_ref[at, :] = dot_nn(value_t, probs_low).T.astype(jnp.bfloat16)


def backward_kernel(factor, peers, *refs):
    parts, (grad_ref, probs_ref) = refs[:peers], refs[peers : peers + 2]
    outs = refs[peers + 2 : 2 * peers + 2]
    dk_sum, dv_sum = refs[2 * peers + 2 :]
    rows = parts[0].shape[1]
    key_t = jnp.concatenate([part[1] for part in parts], axis=0).T
    value = jnp.concatenate([part[2] for part in parts], axis=0)
    for block in range(peers):
        at = pl.ds(block * rows, rows)
        grad = grad_ref[at, :]
        probs_low = probs_ref[0, :, at]
        grad_probs = dot_nt(value, grad)
        probs = probs_low.astype(jnp.float32)
        delta = jnp.sum(probs * grad_probs, axis=0, keepdims=True)
        grad_scores = (probs * (grad_probs - delta)).astype(jnp.bfloat16)
        dv_part = dot_nn(probs_low, grad)
        dk_part = dot_nn(grad_scores, parts[block][0])
        if block == 0:
            dv_sum[...] = dv_part
            dk_sum[...] = dk_part
        else:
            dv_sum[...] += dv_part
            dk_sum[...] += dk_part
        outs[block][0] = (dot_nn(key_t, grad_scores) * factor).T.astype(jnp.bfloat16)
    for block in range(peers):
        at = pl.ds(block * rows, rows)
        outs[block][1] = (dk_sum[at, :] * factor).astype(jnp.bfloat16)
        outs[block][2] = dv_sum[at, :].astype(jnp.bfloat16)


def attention_forward(parts, bias):
    peers = len(parts)
    _, rows, width = parts[0].shape
    heads = width // HEAD_DIM
    total = peers * rows
    pairs = heads * total * total
    return pl.pallas_call(
        functools.partial(forward_kernel, 1.0 / math.sqrt(HEAD_DIM)),
        grid=(heads,),
        in_specs=[pl.BlockSpec((3, rows, HEAD_DIM), lambda h: (0, 0, h))] * peers
        + [pl.BlockSpec((total, total), lambda h: (0, 0))],
        out_specs=[
            pl.BlockSpec((1, total, total), lambda h: (h, 0, 0)),
            pl.BlockSpec((total, HEAD_DIM), lambda h: (0, h)),
        ],
        out_shape=[
            jax.ShapeDtypeStruct((heads, total, total), jnp.bfloat16),
            jax.ShapeDtypeStruct((total, width), jnp.bfloat16),
        ],
        compiler_params=pltpu.CompilerParams(vmem_limit_bytes=VMEM_LIMIT),
        cost_estimate=pl.CostEstimate(
            flops=4 * pairs * HEAD_DIM, bytes_accessed=4 * pairs, transcendentals=pairs
        ),
        name="attention_forward",
    )(*parts, bias)


def attention_backward(parts, grad, probs):
    peers = len(parts)
    _, rows, width = parts[0].shape
    heads = width // HEAD_DIM
    total = peers * rows
    pairs = heads * total * total
    by_part = pl.BlockSpec((3, rows, HEAD_DIM), lambda h: (0, 0, h))
    return pl.pallas_call(
        functools.partial(backward_kernel, 1.0 / math.sqrt(HEAD_DIM), peers),
        grid=(heads,),
        in_specs=[by_part] * peers
        + [pl.BlockSpec((total, HEAD_DIM), lambda h: (0, h))]
        + [pl.BlockSpec((1, total, total), lambda h: (h, 0, 0))],
        out_specs=[by_part] * peers,
        out_shape=[jax.ShapeDtypeStruct((3, rows, width), jnp.bfloat16)] * peers,
        scratch_shapes=[
            pltpu.VMEM((total, HEAD_DIM), jnp.float32),
            pltpu.VMEM((total, HEAD_DIM), jnp.float32),
        ],
        compiler_params=pltpu.CompilerParams(vmem_limit_bytes=VMEM_LIMIT),
        cost_estimate=pl.CostEstimate(
            flops=8 * pairs * HEAD_DIM, bytes_accessed=4 * pairs, transcendentals=0
        ),
        name="attention_backward",
    )(*parts, grad, probs)


def weight_kernel(scale, *refs):
    cots, (att_ref, out_ref) = refs[:-2], refs[-2:]
    cot = jnp.concatenate([cot[...] for cot in cots], axis=0)
    out_ref[...] = (dot_tn(cot, att_ref[...]) * scale).astype(jnp.bfloat16)


def weight_partial(cots, attended, scale):
    rows, features = cots[0].shape
    total, width = attended.shape
    block = 512
    return pl.pallas_call(
        functools.partial(weight_kernel, scale),
        grid=(features // block,),
        in_specs=[pl.BlockSpec((rows, block), lambda i: (0, i))] * len(cots)
        + [pl.BlockSpec((total, width), lambda i: (0, 0))],
        out_specs=pl.BlockSpec((block, width), lambda i: (i, 0)),
        out_shape=jax.ShapeDtypeStruct((features, width), jnp.bfloat16),
        compiler_params=pltpu.CompilerParams(vmem_limit_bytes=VMEM_LIMIT),
        cost_estimate=pl.CostEstimate(
            flops=2 * total * features * width,
            bytes_accessed=2 * features * (total + width),
            transcendentals=0,
        ),
        name="weight_partial",
    )(*cots, attended)


def project_kernel(peers, *refs):
    firsts, seconds, (w_ref, out_ref, total) = refs[:peers], refs[peers : 2 * peers], refs[2 * peers :]
    step = pl.program_id(0)
    width = w_ref.shape[2]
    first = firsts[0].shape[1] // w_ref.shape[0]
    w_first = w_ref[:, :first, :].reshape(firsts[0].shape[1], width)
    w_second = w_ref[:, first:, :].reshape(seconds[0].shape[1], width)
    product = dot_nn(jnp.concatenate([ref[...] for ref in firsts], axis=0), w_first)
    product += dot_nn(jnp.concatenate([ref[...] for ref in seconds], axis=0), w_second)

    @pl.when(step == 0)
    def _():
        total[...] = product

    @pl.when(step > 0)
    def _():
        total[...] += product

    @pl.when(step == pl.num_programs(0) - 1)
    def _():
        out_ref[...] = total[...].astype(jnp.bfloat16)


def project(firsts, seconds, w_all, group):
    peers = len(firsts)
    rows = firsts[0].shape[0]
    owners, depth, width = w_all.shape
    steps = owners // group
    total = peers * rows
    return pl.pallas_call(
        functools.partial(project_kernel, peers),
        grid=(steps,),
        in_specs=[pl.BlockSpec((rows, firsts[0].shape[1] // steps), lambda i: (0, i))] * peers
        + [pl.BlockSpec((rows, seconds[0].shape[1] // steps), lambda i: (0, i))] * peers
        + [pl.BlockSpec((group, depth, width), lambda i: (i, 0, 0))],
        out_specs=pl.BlockSpec((total, width), lambda i: (0, 0)),
        out_shape=jax.ShapeDtypeStruct((total, width), jnp.bfloat16),
        scratch_shapes=[pltpu.VMEM((total, width), jnp.float32)],
        compiler_params=pltpu.CompilerParams(vmem_limit_bytes=VMEM_LIMIT),
        cost_estimate=pl.CostEstimate(
            flops=2 * total * owners * depth * width,
            bytes_accessed=2 * owners * depth * (total + width),
            transcendentals=0,
        ),
        name="project",
    )(*firsts, *seconds, w_all)


def score_bias(tile_pairs, clip_lengths, clip_rows, order):
    tile_count = tile_pairs.shape[0]
    tile_rows = clip_rows // tile_count
    listed = jnp.any(tile_pairs[order][:, :, None] == order[None, None, :], axis=1)
    lengths = jnp.where(listed, clip_lengths[order][None, :], 0)
    live = jnp.arange(tile_rows, dtype=jnp.int32)[None, :, None] < lengths.T[:, None, :]
    bias = jnp.where(live, 0.0, DEAD).astype(jnp.bfloat16).reshape(clip_rows, tile_count)
    return jnp.repeat(bias, tile_rows, axis=1)


def swap(field, step, peers):
    return lax.ppermute(field, "seq", [(i, i ^ step) for i in range(peers)])


def gather_rows(mine, before, after, peers):
    blocks = [mine]
    span = 1
    far = mine
    while span < peers:
        held = mine if span == 1 else lax.optimization_barrier((mine, before))[0]
        far = swap(held, span, peers)
        blocks.append(far)
        if span > 1:
            handed = lax.optimization_barrier((far, after))[0]
            blocks += [swap(handed, step, peers) for step in range(1, span)]
        span *= 2
    return blocks, far


def pairwise_sum(field, before):
    count = field.shape[0]
    position = lax.axis_index("dp")
    bit = 1
    while bit < count:
        pairs = field.reshape((field.shape[0] // 2, 2) + field.shape[1:])
        side = (position // bit) % 2
        kept = lax.dynamic_index_in_dim(pairs, side, 1, keepdims=False)
        sent = lax.dynamic_index_in_dim(pairs, 1 - side, 1, keepdims=False)
        got = lax.ppermute(sent, "dp", [(i, i ^ bit) for i in range(count)])
        if bit == 1:
            got = lax.optimization_barrier((got, before))[0]
        field = (kept.astype(jnp.float32) + got.astype(jnp.float32)).astype(jnp.bfloat16)
        bit *= 2
    return field[0]


def per_device(queries, keys, values, gain_q, gain_k, tile_pairs, tile_lens, out_grad, w_out):
    dp_count = lax.axis_size("dp")
    peers = lax.axis_size("seq")
    position = lax.axis_index("seq")
    me = position.astype(jnp.int32)[None]
    rows = queries.shape[0]
    clip_rows = rows * peers
    tile_count = tile_pairs.shape[0]
    near = tile_count // peers
    depth, width = w_out.shape
    first = depth * 3 // 5
    group = 10 * HEAD_DIM // depth
    w_all = lax.all_gather(w_out, "dp", axis=0, tiled=False)
    sends = prepare(me, queries, keys, values, gain_q, gain_k, peers)
    parts = [sends[0]] + [swap(sends[step], step, peers) for step in range(1, peers)]
    by_owner = out_grad.reshape(rows, dp_count, depth)
    mine_first = by_owner[:, :, :first].reshape(rows, -1)
    mine_second = by_owner[:, :, first:].reshape(rows, -1)
    tiles = jnp.arange(tile_count, dtype=jnp.int32)
    order = ((tiles // near) ^ position) * near + tiles % near
    bias = score_bias(tile_pairs, tile_lens[0], clip_rows, order)
    probs, attended = attention_forward(parts, bias)
    firsts, far_first = gather_rows(mine_first, parts, attended, peers)
    partial_first = weight_partial(firsts, attended, 1.0 / dp_count)
    seconds, far_second = gather_rows(mine_second, far_first, partial_first, peers)
    partial_first = lax.optimization_barrier((partial_first, far_second))[0]
    grad_w_first = lax.psum_scatter(partial_first, "dp", scatter_dimension=0, tiled=True)
    partial_second = weight_partial(seconds, attended, 1.0 / dp_count)
    grad = project(firsts, seconds, w_all, group)
    backs = attention_backward(parts, grad, probs)
    grad_w_second = pairwise_sum(partial_second.reshape(dp_count, depth - first, width), backs)
    backs = [backs[0]] + [swap(backs[step], step, peers) for step in range(1, peers)]
    grad_q, grad_k, grad_v = finish(me, queries, keys, gain_q, gain_k, backs)
    grad_w = jnp.concatenate([grad_w_first, grad_w_second], axis=0)
    return (grad_q, grad_k, grad_v, grad_w.astype(jnp.float32))


def solution(mesh):
    return jax.shard_map(
        per_device,
        mesh=mesh,
        in_specs=(
            P(("dp", "seq"), None),
            P(("dp", "seq"), None),
            P(("dp", "seq"), None),
            P(),
            P(),
            P(),
            P("dp", None),
            P(("dp", "seq"), None),
            P("dp", "seq"),
        ),
        out_specs=(
            P(("dp", "seq"), None),
            P(("dp", "seq"), None),
            P(("dp", "seq"), None),
            P("dp", "seq"),
        ),
        check_vma=False,
    )
```
